512 devices in a mesh: dp: 32 (over x, z_lo), tensor: 16 (over z_hi, y, core).
Axes of the slice: x: 4, y: 4, z: 16 (z_hi: 2, z_lo: 8; z = z_hi * 8 + z_lo), core: 2. Of those that a mesh axis runs over, the one named last changes fastest.
Arguments:
- tokens: bfloat16 [64, 256, 6144], P('dp', None, 'tensor'), may hold values from -6 to 6
- mix_weight: int32 [64], P('dp'), may hold values from 0 to 256
- partner_offset: int32 [64], P('dp'), may hold values from 0 to 1
- ln_gain: float32 [6144], replicated, may hold values from 0.25 to 1.75
- qkv_weight: bfloat16 [3, 6144, 4096], P(None, 'dp', 'tensor'), may hold values from -0.05103104 to 0.05103104
- qk_gain: float32 [2, 4096], P(None, 'tensor'), may hold values from 0.6 to 5
Outputs:
- attended: bfloat16 [64, 256, 4096], P('dp', None, 'tensor')
The draws below stay inside these ranges and needn't reach their ends.
All inputs are finite; a program needn't handle non-finite values.
Results may differ from the reference program's by a relative error of at most 0.012.
The reference program's roundings to bfloat16 on the way count: a program that leaves them out, or rounds other values in their place, can miss the bound.
Values may be sent and summed in bfloat16 or wider, within the bound.
No kernel may reach another device: no remote copies, remote signals or barrier semaphores. Data moves between devices by JAX's collectives and lax.ppermute only.
A program may use at most 64 MiB of HBM per device.

```python
import jax
import jax.numpy as jnp
from jax import lax

D = 6144
HEADS = 32
HEAD = 128
PATCHES = 256
IMGS = 2
IMAGES = 64
N_DP = 32


def draw_qkv_weight(key, part):
    key = jax.random.fold_in(key, 11)
    bound = 4.0 * D ** (-0.5)
    base = jnp.clip(jax.random.normal(key, (3, D, HEADS * HEAD), jnp.float32) * D ** (-0.5), -bound, bound)
    return base.astype(jnp.bfloat16)


def draw_qk_gain(key, part):
    key = jax.random.fold_in(key, 12)
    unit = jax.random.uniform(key, (2, HEADS * HEAD), jnp.float32)
    return 0.6 + 1.2 * unit


def place_ends(array, own_key, low, largest):
    place = [jax.random.randint(jax.random.fold_in(own_key, axis), (), 0, length) for axis, length in enumerate(array.shape)]
    main_axis = array.shape.index(max(array.shape))
    beside = place[:main_axis] + [(place[main_axis] + 1) % array.shape[main_axis]] + place[main_axis + 1:]
    return array.at[tuple(place)].set(low).at[tuple(beside)].set(largest)


def levels(own_key, dims, cuts, smallest, largest):
    def one(dim, blocks):
        draws = jax.random.uniform(jax.random.fold_in(jax.random.fold_in(own_key, 6), dim), (blocks,), jnp.float32, smallest / len(cuts), largest / len(cuts))
        return jnp.repeat(jnp.exp(draws), dims[dim] // blocks).reshape((-1,) + (1,) * (len(dims) - dim - 1))

    loudness = one(*cuts[0])
    for cut in cuts[1:]:
        loudness = loudness * one(*cut)
    return loudness


def bell_draw(rng, shape, width, most, pieces=(), kind=jnp.bfloat16):
    gain = levels(rng, shape, pieces, -0.22, 0.18) if pieces else 1.0
    entries = jax.random.normal(rng, shape, jnp.float32) * width * gain
    return jnp.minimum(jnp.maximum(entries, -most), most).astype(kind)


def setup_inputs(seed: int = 0) -> dict:
    key_list = jax.random.split(jax.random.key(seed), 7)
    tokens = bell_draw(key_list[0], (IMAGES, PATCHES, D), 1.0, 6.0, ((0, 32), (2, 16)))
    mix_weight = place_ends(jax.random.randint(key_list[1], (IMAGES,), 0, 257), jax.random.fold_in(key_list[1], 1), 0, 256).astype(jnp.int32)
    partner_offset = place_ends(jax.random.randint(key_list[2], (IMAGES,), 0, IMGS), jax.random.fold_in(key_list[2], 1), 0, IMGS - 1).astype(jnp.int32)
    ln_gain = jnp.clip(1.0 + 0.15 * jax.random.normal(key_list[3], (D,), jnp.float32), 0.25, 1.75)
    qkv_weight = draw_qkv_weight(jax.random.fold_in(key_list[6], 71), 0)
    qk_gain = draw_qk_gain(jax.random.fold_in(key_list[6], 71), 0)
    return dict(tokens=tokens, mix_weight=mix_weight, partner_offset=partner_offset, ln_gain=ln_gain, qkv_weight=qkv_weight, qk_gain=qk_gain)


def norm_last(values, eps):
    mean = lax.optimization_barrier(jnp.mean(values, axis=-1, keepdims=True))
    centred = values - mean
    var = lax.optimization_barrier(jnp.mean(centred * centred, axis=-1, keepdims=True))
    return centred / jnp.sqrt(var + eps)

def reference(tokens, mix_weight, partner_offset, ln_gain, qkv_weight, qk_gain):
    images = tokens.shape[0]
    index = jnp.arange(images, dtype=jnp.int32)
    partner_index = (index // IMGS + 1) % N_DP * IMGS + (index % IMGS + partner_offset.astype(jnp.int32)) % IMGS
    partner = jnp.take(tokens, partner_index.astype(jnp.int32), axis=0)
    lam = mix_weight.astype(jnp.float32) / 256.0
    mixed = lam[:, None, None] * tokens.astype(jnp.float32) + (1.0 - lam)[:, None, None] * partner.astype(jnp.float32)
    mixed = mixed.astype(jnp.bfloat16)
    normed = (norm_last(mixed.astype(jnp.float32), 1e-06) * ln_gain).astype(jnp.bfloat16)
    scale = HEAD ** (-0.5)

    def one_image(rows):
        query = jnp.dot(rows, qkv_weight[0], preferred_element_type=jnp.float32).astype(jnp.bfloat16)
        keys = jnp.dot(rows, qkv_weight[1], preferred_element_type=jnp.float32).astype(jnp.bfloat16)
        values = jnp.dot(rows, qkv_weight[2], preferred_element_type=jnp.float32).astype(jnp.bfloat16)
        query = query.astype(jnp.float32).reshape(PATCHES, HEADS, HEAD)
        keys = keys.astype(jnp.float32).reshape(PATCHES, HEADS, HEAD)
        values = values.astype(jnp.float32).reshape(PATCHES, HEADS, HEAD)
        q_norm = (norm_last(query, 1e-06) * qk_gain[0].reshape(HEADS, HEAD) * scale).astype(jnp.bfloat16)
        k_norm = (norm_last(keys, 1e-06) * qk_gain[1].reshape(HEADS, HEAD)).astype(jnp.bfloat16)
        scores = jnp.einsum('phe,qhe->hpq', q_norm.astype(jnp.float32), k_norm.astype(jnp.float32))
        probs = jax.nn.softmax(scores, axis=-1).astype(jnp.bfloat16)
        output = jnp.einsum('hpq,qhe->phe', probs.astype(jnp.float32), values)
        return output.astype(jnp.bfloat16).reshape(PATCHES, HEADS * HEAD)
    return lax.map(one_image, normed)
```

```python
import jax
import jax.numpy as jnp
from jax import lax
from jax.sharding import Mesh, PartitionSpec as P

HEAD = 128
AXES = ("x", "zl", "zh", "y", "c")
SIZES = (4, 8, 2, 4, 2)


def move(value, target):
    pairs = []
    for source in range(512):
        c = source % 2
        y = source // 2 % 4
        zh = source // 8 % 2
        zl = source // 16 % 8
        x = source // 128
        goal = target(x, zl, zh, y, c)
        if goal is None:
            continue
        gx, gzl, gzh, gy, gc = goal
        pairs.append((source, (((gx % 4 * 8 + gzl) * 2 + gzh) * 4 + gy % 4) * 2 + gc))
    return lax.ppermute(value, AXES, pairs)


def along_x(value, by):
    return move(value, lambda x, zl, zh, y, c: (x + by, zl, zh, y, c))


def along_y(value, by):
    return move(value, lambda x, zl, zh, y, c: (x, zl, zh, y + by, c))


def along_z(value, by):
    def target(x, zl, zh, y, c):
        z = (zh * 8 + zl + by) % 16
        return x, z % 8, z // 8, y, c

    return move(value, target)


def other_core(value):
    return move(value, lambda x, zl, zh, y, c: (x, zl, zh, y, 1 - c))


def previous_images(value):
    def target(x, zl, zh, y, c):
        dp = (x * 8 + zl - 1) % 32
        return dp // 8, dp % 8, zh, y, c

    return move(value, target)


def norm_last(values, eps):
    mean = jnp.mean(values, axis=-1, keepdims=True)
    centred = values - mean
    var = jnp.mean(centred * centred, axis=-1, keepdims=True)
    return centred / jnp.sqrt(var + eps)


def ring_of_four(value, shift, axis):
    size = value.shape[axis] // 2
    low, high = lax.slice_in_dim(value, 0, size, axis=axis), lax.slice_in_dim(value, size, 2 * size, axis=axis)
    from_left = shift(value, 1)
    from_right = shift(value, -1)
    low = shift(lax.slice_in_dim(from_left, 0, size, axis=axis), 1)
    high = shift(lax.slice_in_dim(from_right, size, 2 * size, axis=axis), -1)
    opposite = jnp.concatenate([low, high], axis=axis)
    return value, from_right, opposite, from_left


def gather_tokens(mixed):
    ahead = along_z(along_z(mixed[0], 4), 4)
    behind = along_z(along_z(mixed[1], -4), -4)
    other = jnp.stack([ahead, behind])
    zh, y, c = lax.axis_index("zh"), lax.axis_index("y"), lax.axis_index("c")
    both = jnp.where(zh == 0, jnp.stack([mixed, other]), jnp.stack([other, mixed]))
    column = jnp.stack(ring_of_four(both, along_y, 1))
    column = jnp.take(column, (jnp.arange(4) - y) % 4, axis=0)
    across = other_core(column)
    cores = jnp.where(c == 0, jnp.stack([column, across]), jnp.stack([across, column]))
    return cores.transpose(3, 4, 2, 1, 0, 5).reshape(2, 256, 6144)


def per_device(tokens, mix_weight, partner_offset, ln_gain, qkv_weight, qk_gain):
    images = tokens.shape[0]
    quarter = lax.all_gather(qkv_weight, "zl", axis=1, tiled=True)
    partner_block = previous_images(tokens)
    local_index = (jnp.arange(images, dtype=jnp.int32) + partner_offset) % images
    partner = jnp.take(partner_block, local_index, axis=0)
    lam = mix_weight.astype(jnp.float32) / 256.0
    mixed = lam[:, None, None] * tokens.astype(jnp.float32) + (1.0 - lam)[
        :, None, None
    ] * partner.astype(jnp.float32)
    mixed = mixed.astype(jnp.bfloat16)
    mixed_all = gather_tokens(mixed)
    normed = (norm_last(mixed_all.astype(jnp.float32), 1e-06) * ln_gain).astype(jnp.bfloat16)
    width_dev = qkv_weight.shape[2]
    patches = normed.shape[1]
    x = lax.axis_index("x")
    projected = 0.0
    for step, weight in enumerate(ring_of_four(quarter, along_x, 1)):
        rows = lax.dynamic_slice_in_dim(normed, (x + step) % 4 * 1536, 1536, axis=2)
        projected = projected + jnp.einsum(
            "ipd,cde->cipe", rows, weight, preferred_element_type=jnp.float32
        )
    qkv = projected.astype(jnp.bfloat16)
    heads_dev = width_dev // HEAD
    query = qkv[0].astype(jnp.float32).reshape(images, patches, heads_dev, HEAD)
    keys = qkv[1].astype(jnp.float32).reshape(images, patches, heads_dev, HEAD)
    values = qkv[2].reshape(images, patches, heads_dev, HEAD)
    q_norm = (
        norm_last(query, 1e-06) * qk_gain[0].reshape(heads_dev, HEAD) * HEAD ** (-0.5)
    ).astype(jnp.bfloat16)
    k_norm = (norm_last(keys, 1e-06) * qk_gain[1].reshape(heads_dev, HEAD)).astype(jnp.bfloat16)
    scores = jnp.einsum("iphe,iqhe->ihpq", q_norm, k_norm, preferred_element_type=jnp.float32)
    probs = jax.nn.softmax(scores, axis=-1).astype(jnp.bfloat16)
    output = jnp.einsum("ihpq,iqhe->iphe", probs, values, preferred_element_type=jnp.float32)
    return output.astype(jnp.bfloat16).reshape(images, patches, width_dev)


def solution(mesh):
    grid = Mesh(mesh.devices.reshape(SIZES), AXES)
    dp, tensor = ("x", "zl"), ("zh", "y", "c")
    placed = (
        P(dp, None, tensor),
        P(dp),
        P(dp),
        P(),
        P(None, dp, tensor),
        P(None, tensor),
    )
    return jax.shard_map(
        per_device, mesh=grid, in_specs=placed, out_specs=P(dp, None, tensor), check_vma=False
    )
```

```python
import functools

import jax
import jax.numpy as jnp
import numpy as np
from jax import lax
from jax.experimental import pallas as pl
from jax.experimental.pallas import tpu as pltpu
from jax.sharding import Mesh, PartitionSpec as P

HEAD = 128
AXES = ("x", "zl", "zh", "y", "c")
SIZES = (4, 8, 2, 4, 2)
VMEM_LIMIT = 56 * 1024 * 1024

SLOT_SOURCES = np.array(
    [
        [0, 2, 1, 3, 4, 5, 6, 7],
        [1, 0, 2, 4, 3, 5, 6, 7],
        [2, 1, 3, 0, 4, 6, 7, 5],
        [3, 2, 4, 1, 5, 7, 6, 0],
        [4, 3, 5, 2, 6, 0, 1, 7],
        [5, 4, 6, 3, 7, 1, 0, 2],
        [6, 5, 7, 4, 3, 2, 1, 0],
        [7, 6, 5, 3, 4, 2, 1, 0],
    ],
    dtype=np.int32,
)


def move(value, target):
    pairs = []
    for source in range(512):
        c = source % 2
        y = source // 2 % 4
        zh = source // 8 % 2
        zl = source // 16 % 8
        x = source // 128
        goal = target(x, zl, zh, y, c)
        if goal is None:
            continue
        gx, gzl, gzh, gy, gc = goal
        pairs.append((source, (((gx % 4 * 8 + gzl) * 2 + gzh) * 4 + gy % 4) * 2 + gc))
    return lax.ppermute(value, AXES, pairs)


def along_x(value, by):
    return move(value, lambda x, zl, zh, y, c: (x + by, zl, zh, y, c))


def along_z(value, by):
    def target(x, zl, zh, y, c):
        z = (zh * 8 + zl + by) % 16
        return x, z % 8, z // 8, y, c

    return move(value, target)


def along_line(value, up=(), down=()):
    def target(x, zl, zh, y, c):
        if zl in up:
            return x, zl + 1, zh, y, c
        if zl in down:
            return x, zl - 1, zh, y, c
        return None

    return move(value, target)


def previous_images(value):
    def target(x, zl, zh, y, c):
        dp = (x * 8 + zl - 1) % 32
        return dp // 8, dp % 8, zh, y, c

    return move(value, target)


def norm_last(values, eps):
    mean = jnp.mean(values, axis=-1, keepdims=True)
    centred = values - mean
    var = jnp.mean(centred * centred, axis=-1, keepdims=True)
    return centred / jnp.sqrt(var + eps)


def norm_kernel(own_ref, other_ref, gain_ref, out_ref):
    parts = [ref[j].astype(jnp.float32) for ref in (own_ref, other_ref) for j in range(8)]
    count = 16 * parts[0].shape[1]
    total = functools.reduce(jnp.add, parts)
    mean = jnp.sum(total, axis=-1, keepdims=True) / count
    parts = [part - mean for part in parts]
    total = functools.reduce(jnp.add, [part * part for part in parts])
    scale = 1.0 / jnp.sqrt(jnp.sum(total, axis=-1, keepdims=True) / count + 1e-06)
    for block, part in enumerate(parts):
        normed = (part * scale * gain_ref[block : block + 1, :]).astype(jnp.bfloat16)
        out_ref[block] = normed[:, :192]
        out_ref[16 + block] = normed[:, 192:]


def norm_tokens(own, other, gain):
    rows = 64
    return pl.pallas_call(
        norm_kernel,
        out_shape=jax.ShapeDtypeStruct((32, 512, 192), jnp.bfloat16),
        grid=(512 // rows,),
        in_specs=[
            pl.BlockSpec((8, rows, 384), lambda i: (0, i, 0)),
            pl.BlockSpec((8, rows, 384), lambda i: (0, i, 0)),
            pl.BlockSpec((16, 384), lambda i: (0, 0)),
        ],
        out_specs=pl.BlockSpec((32, rows, 192), lambda i: (0, i, 0)),
        compiler_params=pltpu.CompilerParams(vmem_limit_bytes=VMEM_LIMIT),
        cost_estimate=pl.CostEstimate(
            flops=512 * 6144 * 8, bytes_accessed=14 * 2**20, transcendentals=0
        ),
    )(own, other, gain)


def add_products(blocks, index_ref, normed_ref, piece_refs, acc_ref):
    for which, (left, right) in blocks:
        rows = normed_ref[index_ref[which]]
        for c in range(3):
            weight = jnp.concatenate(
                [piece_refs[left[0]][left[1], c], piece_refs[right[0]][right[1], c]], axis=-1
            )
            acc_ref[c] += jnp.dot(rows, weight, preferred_element_type=jnp.float32)


def first_kernel(blocks, index_ref, normed_ref, *refs):
    pieces, acc_ref = refs[:-1], refs[-1]
    acc_ref[...] = jnp.zeros_like(acc_ref)
    add_products(blocks, index_ref, normed_ref, pieces, acc_ref)


def next_kernel(blocks, index_ref, normed_ref, held_ref, *refs):
    pieces, acc_ref = refs[:-1], refs[-1]
    acc_ref[...] = held_ref[...]
    add_products(blocks, index_ref, normed_ref, pieces, acc_ref)


def attend(acc_ref, gain_ref, out_ref):
    for head in range(2):
        columns = slice(head * HEAD, (head + 1) * HEAD)
        for image in range(2):
            rows = slice(image * 256, (image + 1) * 256)
            query, keys, values = (
                acc_ref[c, rows, columns].astype(jnp.bfloat16) for c in range(3)
            )
            q_norm = (
                norm_last(query.astype(jnp.float32), 1e-06)
                * gain_ref[0:1, columns]
                * HEAD ** (-0.5)
            ).astype(jnp.bfloat16)
            k_norm = (
                norm_last(keys.astype(jnp.float32), 1e-06) * gain_ref[1:2, columns]
            ).astype(jnp.bfloat16)
            scores = lax.dot_general(
                q_norm, k_norm, (((1,), (1,)), ((), ())), preferred_element_type=jnp.float32
            )
            raised = jnp.exp(scores - jnp.max(scores, axis=-1, keepdims=True))
            probs = (raised / jnp.sum(raised, axis=-1, keepdims=True)).astype(jnp.bfloat16)
            out_ref[rows, columns] = jnp.dot(
                probs, values, preferred_element_type=jnp.float32
            ).astype(jnp.bfloat16)


def last_kernel(blocks, index_ref, normed_ref, held_ref, gain_ref, *refs):
    pieces, out_ref, acc_ref = refs[:-2], refs[-2], refs[-1]
    acc_ref[...] = held_ref[...]
    add_products(blocks, index_ref, normed_ref, pieces, acc_ref)
    attend(acc_ref, gain_ref, out_ref)


def project(kernel, blocks, index, normed, extra, pieces, out_shape, scratch=()):
    whole = pl.BlockSpec(memory_space=pltpu.VMEM)
    return pl.pallas_call(
        functools.partial(kernel, blocks),
        out_shape=out_shape,
        in_specs=[pl.BlockSpec(memory_space=pltpu.SMEM)] + [whole] * (1 + len(extra) + len(pieces)),
        out_specs=whole,
        scratch_shapes=list(scratch),
        compiler_params=pltpu.CompilerParams(vmem_limit_bytes=VMEM_LIMIT),
        cost_estimate=pl.CostEstimate(
            flops=len(blocks) * 512 * 192 * 768 * 2,
            bytes_accessed=8 * 2**20 + len(blocks) * 294912,
            transcendentals=0,
        ),
    )(index, normed, *extra, *pieces)


def weight_slots(own, zl):
    a1 = along_line(own, up=range(0, 7))
    b1 = along_line(own, down=range(1, 8))
    a2 = along_line(a1, up=range(1, 7))
    b2 = along_line(b1, down=range(1, 7))
    a3 = along_line(a2, up=range(2, 7))
    b3 = along_line(b2, down=range(1, 6))
    a4 = along_line(a3, up=range(3, 7))
    b4 = along_line(b3, down=range(1, 5))
    m4 = jnp.where(zl >= 4, a4, b4)
    m5 = along_line(m4, up=range(4, 7), down=range(1, 4))
    m6 = along_line(m5, up=range(5, 7), down=range(1, 3))
    m7 = along_line(m6, up=(6,), down=(1,))
    end = (zl == 0) | (zl == 7)
    second = (zl == 1) | (zl == 6)
    return [
        own,
        jnp.where(zl == 0, b2, a1),
        jnp.where(zl == 7, a2, b1),
        jnp.where(zl <= 1, b3, jnp.where(zl == 7, m4, a2)),
        jnp.where(zl == 0, m4, jnp.where(zl <= 5, b2, a3)),
        jnp.where(end, m5, m4),
        jnp.where(end, m6, jnp.where(zl == 3, b3, jnp.where(zl == 4, a3, m5))),
        jnp.where(
            end, m7, jnp.where(second, m6, jnp.where((zl == 2) | (zl == 4), b3, a3))
        ),
    ]


def per_device(tokens, mix_weight, partner_offset, ln_gain, qkv_weight, qk_gain):
    x, zl, zh = lax.axis_index("x"), lax.axis_index("zl"), lax.axis_index("zh")

    partner_block = previous_images(tokens)
    lam = (mix_weight.astype(jnp.float32) / 256.0)[:, None, None]
    first = ((jnp.arange(2, dtype=jnp.int32) + partner_offset) % 2 == 0)[:, None, None]
    partner = jnp.where(first, partner_block[0], partner_block[1])
    mixed = lam * tokens.astype(jnp.float32) + (1.0 - lam) * partner.astype(jnp.float32)
    mixed = mixed.astype(jnp.bfloat16)

    ahead = along_z(along_z(mixed[0], 4), 4)
    behind = along_z(along_z(mixed[1], -4), -4)
    own_features = lax.all_gather(mixed.reshape(512, 384), ("y", "c"))
    other_features = lax.all_gather(jnp.concatenate([ahead, behind]), ("y", "c"))

    halves = jnp.stack([qkv_weight[:, :, :HEAD], qkv_weight[:, :, HEAD:]])
    slots = weight_slots(halves, zl)
    own, left, right = [], [], []
    for group in ((0,), (1, 2), (3, 4), (5, 6), (7,)):
        block = jnp.concatenate([slots[slot] for slot in group])
        to_right, to_left = [block], [block]
        if left:
            full = left[-1].shape[0] // 2 * 2 if len(left) == 1 else 4
            for start in range(0, full, 2):
                to_right.append(left[-1][start : start + 1])
                to_left.append(right[-1][start + 1 : start + 2])
        own.append(block)
        left.append(along_x(jnp.concatenate(to_right), 1))
        right.append(along_x(jnp.concatenate(to_left), -1))
    last_left = along_x(left[-1][0:1], 1)
    last_right = along_x(right[-1][1:2], -1)

    sources = jnp.asarray(SLOT_SOURCES)[zl]
    block_of = ((x + jnp.arange(4, dtype=jnp.int32)) % 4 * 8)[:, None] + sources[None, :]
    feature = block_of // 2
    index = block_of % 2 * 16 + (feature // 8 + zh) % 2 * 8 + feature % 8
    index = index.reshape(32).astype(jnp.int32)

    gain = ln_gain.reshape(2, 8, 384)
    gain = jnp.where(zh == 0, gain, gain[::-1]).reshape(16, 384)
    normed = norm_tokens(own_features, other_features, gain)

    def three(slot, place):
        return [
            (slot, ((0, 2 * place), (0, 2 * place + 1))),
            (8 + slot, ((2, 2 * place), (2, 2 * place + 1))),
            (24 + slot, ((1, 2 * place), (1, 2 * place + 1))),
        ]

    def at(blocks, base):
        return [
            (which, ((a[0] + base, a[1]), (b[0] + base, b[1]))) for which, (a, b) in blocks
        ]

    first_blocks, pieces = [], []
    for group, (slots_in, opposite) in enumerate(
        [((0,), ()), ((1, 2), (0,)), ((3, 4), (1, 2)), ((5, 6), (3, 4))]
    ):
        blocks = []
        for place, slot in enumerate(slots_in):
            blocks += three(slot, place)
        for place, slot in enumerate(opposite):
            tail = 2 * len(slots_in) + place
            blocks.append((16 + slot, ((1, tail), (2, tail))))
        first_blocks += at(blocks, 3 * group)
        pieces += [own[group], left[group], right[group]]
    acc_shape = jax.ShapeDtypeStruct((3, 512, 256), jnp.float32)
    acc = project(first_kernel, first_blocks, index, normed, [], pieces, acc_shape)
    blocks = three(7, 0) + [(16 + 5, ((1, 2), (2, 2))), (16 + 6, ((1, 3), (2, 3)))]
    acc = project(
        next_kernel, blocks, index, normed, [acc], [own[4], left[4], right[4]], acc_shape
    )
    out = project(
        last_kernel,
        [(16 + 7, ((0, 0), (1, 0)))],
        index,
        normed,
        [acc, qk_gain],
        [last_left, last_right],
        jax.ShapeDtypeStruct((512, 256), jnp.bfloat16),
        [pltpu.VMEM((3, 512, 256), jnp.float32)],
    )
    return out.reshape(2, 256, 256)


def solution(mesh):
    grid = Mesh(mesh.devices.reshape(SIZES), AXES)
    dp, tensor = ("x", "zl"), ("zh", "y", "c")
    placed = (
        P(dp, None, tensor),
        P(dp),
        P(dp),
        P(),
        P(None, dp, tensor),
        P(None, tensor),
    )
    return jax.shard_map(
        per_device, mesh=grid, in_specs=placed, out_specs=P(dp, None, tensor), check_vma=False
    )
```

```python
import functools

import jax
import jax.numpy as jnp
import numpy as np
from jax import lax
from jax.experimental import pallas as pl
from jax.experimental.pallas import tpu as pltpu
from jax.sharding import Mesh, PartitionSpec as P

HEAD = 128
AXES = ("x", "zl", "zh", "y", "c")
SIZES = (4, 8, 2, 4, 2)
VMEM_LIMIT = 32 * 1024 * 1024

SLOT_SOURCES = np.array(
    [
        [0, 2, 1, 3, 4, 5, 6, 7],
        [1, 0, 2, 4, 3, 5, 6, 7],
        [2, 1, 3, 0, 4, 6, 7, 5],
        [3, 2, 4, 1, 5, 7, 6, 0],
        [4, 3, 5, 2, 6, 0, 1, 7],
        [5, 4, 6, 3, 7, 1, 0, 2],
        [6, 5, 7, 4, 3, 2, 1, 0],
        [7, 6, 5, 3, 4, 2, 1, 0],
    ],
    dtype=np.int32,
)


def move(value, target):
    pairs = []
    for source in range(512):
        c = source % 2
        y = source // 2 % 4
        zh = source // 8 % 2
        zl = source // 16 % 8
        x = source // 128
        goal = target(x, zl, zh, y, c)
        if goal is None:
            continue
        gx, gzl, gzh, gy, gc = goal
        pairs.append((source, (((gx % 4 * 8 + gzl) * 2 + gzh) * 4 + gy % 4) * 2 + gc))
    return lax.ppermute(value, AXES, pairs)


def along_x(value, by):
    return move(value, lambda x, zl, zh, y, c: (x + by, zl, zh, y, c))


def along_z(value, by):
    def target(x, zl, zh, y, c):
        z = (zh * 8 + zl + by) % 16
        return x, z % 8, z // 8, y, c

    return move(value, target)


def along_line(value, up=(), down=()):
    def target(x, zl, zh, y, c):
        if zl in up:
            return x, zl + 1, zh, y, c
        if zl in down:
            return x, zl - 1, zh, y, c
        return None

    return move(value, target)


def previous_images(value):
    def target(x, zl, zh, y, c):
        dp = (x * 8 + zl - 1) % 32
        return dp // 8, dp % 8, zh, y, c

    return move(value, target)


def norm_last(values, eps):
    mean = jnp.mean(values, axis=-1, keepdims=True)
    centred = values - mean
    var = jnp.mean(centred * centred, axis=-1, keepdims=True)
    return centred / jnp.sqrt(var + eps)


def norm_kernel(own_ref, other_ref, gain_ref, out_ref):
    parts = [ref[j].astype(jnp.float32) for ref in (own_ref, other_ref) for j in range(8)]
    count = 16 * parts[0].shape[1]
    total = functools.reduce(jnp.add, parts)
    mean = jnp.sum(total, axis=-1, keepdims=True) / count
    parts = [part - mean for part in parts]
    total = functools.reduce(jnp.add, [part * part for part in parts])
    scale = 1.0 / jnp.sqrt(jnp.sum(total, axis=-1, keepdims=True) / count + 1e-06)
    for block, part in enumerate(parts):
        normed = (part * scale * gain_ref[block : block + 1, :]).astype(jnp.bfloat16)
        out_ref[block] = normed[:, :192]
        out_ref[16 + block] = normed[:, 192:]


def norm_tokens(own, other, gain):
    rows = 64
    return pl.pallas_call(
        norm_kernel,
        out_shape=jax.ShapeDtypeStruct((32, 512, 192), jnp.bfloat16),
        grid=(512 // rows,),
        in_specs=[
            pl.BlockSpec((8, rows, 384), lambda i: (0, i, 0)),
            pl.BlockSpec((8, rows, 384), lambda i: (0, i, 0)),
            pl.BlockSpec((16, 384), lambda i: (0, 0)),
        ],
        out_specs=pl.BlockSpec((32, rows, 192), lambda i: (0, i, 0)),
        compiler_params=pltpu.CompilerParams(vmem_limit_bytes=VMEM_LIMIT),
        cost_estimate=pl.CostEstimate(
            flops=512 * 6144 * 8, bytes_accessed=14 * 2**20, transcendentals=0
        ),
    )(own, other, gain)


def add_products(blocks, index_ref, normed_ref, piece_refs, acc_ref):
    for which, (left, right) in blocks:
        rows = normed_ref[index_ref[which]]
        for c in range(3):
            weight = jnp.concatenate(
                [piece_refs[left[0]][left[1], c], piece_refs[right[0]][right[1], c]], axis=-1
            )
            acc_ref[c] += jnp.dot(rows, weight, preferred_element_type=jnp.float32)


def first_kernel(blocks, index_ref, normed_ref, *refs):
    pieces, acc_ref = refs[:-1], refs[-1]
    acc_ref[...] = jnp.zeros_like(acc_ref)
    add_products(blocks, index_ref, normed_ref, pieces, acc_ref)


def next_kernel(blocks, index_ref, normed_ref, held_ref, *refs):
    pieces, acc_ref = refs[:-1], refs[-1]
    acc_ref[...] = held_ref[...]
    add_products(blocks, index_ref, normed_ref, pieces, acc_ref)


def attend(acc_ref, gain_ref, out_ref):
    for head in range(2):
        columns = slice(head * HEAD, (head + 1) * HEAD)
        for image in range(2):
            rows = slice(image * 256, (image + 1) * 256)
            query, keys, values = (
                acc_ref[c, rows, columns].astype(jnp.bfloat16) for c in range(3)
            )
            q_norm = (
                norm_last(query.astype(jnp.float32), 1e-06)
                * gain_ref[0:1, columns]
                * HEAD ** (-0.5)
            ).astype(jnp.bfloat16)
            k_norm = (
                norm_last(keys.astype(jnp.float32), 1e-06) * gain_ref[1:2, columns]
            ).astype(jnp.bfloat16)
            scores = lax.dot_general(
                q_norm, k_norm, (((1,), (1,)), ((), ())), preferred_element_type=jnp.float32
            )
            raised = jnp.exp(scores - jnp.max(scores, axis=-1, keepdims=True))
            probs = (raised / jnp.sum(raised, axis=-1, keepdims=True)).astype(jnp.bfloat16)
            out_ref[rows, columns] = jnp.dot(
                probs, values, preferred_element_type=jnp.float32
            ).astype(jnp.bfloat16)


def last_kernel(blocks, index_ref, normed_ref, held_ref, gain_ref, *refs):
    pieces, out_ref, acc_ref = refs[:-2], refs[-2], refs[-1]
    acc_ref[...] = held_ref[...]
    add_products(blocks, index_ref, normed_ref, pieces, acc_ref)
    attend(acc_ref, gain_ref, out_ref)


def project(kernel, blocks, index, normed, extra, pieces, out_shape, scratch=()):
    whole = pl.BlockSpec(memory_space=pltpu.VMEM)
    return pl.pallas_call(
        functools.partial(kernel, blocks),
        out_shape=out_shape,
        in_specs=[pl.BlockSpec(memory_space=pltpu.SMEM)] + [whole] * (1 + len(extra) + len(pieces)),
        out_specs=whole,
        scratch_shapes=list(scratch),
        compiler_params=pltpu.CompilerParams(vmem_limit_bytes=VMEM_LIMIT),
        cost_estimate=pl.CostEstimate(
            flops=len(blocks) * 512 * 192 * 768 * 2,
            bytes_accessed=8 * 2**20 + len(blocks) * 294912,
            transcendentals=0,
        ),
    )(index, normed, *extra, *pieces)


def relay_kernel(slots, forward, zl_ref, *refs):
    *sources, left_ref, right_ref, to_right, to_left = refs
    zl = zl_ref[0]
    for place, choices in enumerate(slots):
        for source, rows in choices:
            chosen = functools.reduce(jnp.logical_or, [zl == row for row in rows])

            @pl.when(chosen)
            def _(source=source, place=place):
                block = sources[source][...]
                to_right[2 * place : 2 * place + 2] = block
                to_left[2 * place : 2 * place + 2] = block

    for place in range(forward):
        to_right[2 * len(slots) + place] = left_ref[2 * place]
        to_left[2 * len(slots) + place] = right_ref[2 * place + 1]


def relay(zl, slots, arrays, left, right, forward):
    whole = pl.BlockSpec(memory_space=pltpu.VMEM)
    message = jax.ShapeDtypeStruct((2 * len(slots) + forward, 3, 192, HEAD), jnp.bfloat16)
    return pl.pallas_call(
        functools.partial(relay_kernel, slots, forward),
        out_shape=(message, message),
        in_specs=[pl.BlockSpec(memory_space=pltpu.SMEM)] + [whole] * (len(arrays) + 2),
        out_specs=(whole, whole),
        compiler_params=pltpu.CompilerParams(vmem_limit_bytes=16 * 2**20),
        cost_estimate=pl.CostEstimate(flops=0, bytes_accessed=4 * 2**20, transcendentals=0),
    )(zl, *arrays, left, right)


def gather_weights(own, zl):
    row = zl.reshape(1)
    left, right, sent = [along_x(own, 1)], [along_x(own, -1)], [(own, own)]

    def group(slots, arrays):
        forward = left[-1].shape[0] // 2 if len(left) == 1 else 2
        to_right, to_left = relay(row, slots, arrays, left[-1], right[-1], forward)
        sent.append((to_right, to_left))
        left.append(along_x(to_right, 1))
        right.append(along_x(to_left, -1))

    a1 = along_line(own, up=range(0, 7))
    b1 = along_line(own, down=range(1, 8))
    a2 = along_line(a1, up=range(1, 7))
    b2 = along_line(b1, down=range(1, 7))
    group(
        [[(0, range(1, 8)), (3, (0,))], [(1, range(0, 7)), (2, (7,))]],
        [a1, b1, a2, b2],
    )
    a3 = along_line(a2, up=range(2, 7))
    b3 = along_line(b2, down=range(1, 6))
    a4 = along_line(a3, up=range(3, 7))
    b4 = along_line(b3, down=range(1, 5))
    m4 = jnp.where(zl >= 4, a4, b4)
    group(
        [
            [(0, range(2, 7)), (3, (0, 1)), (4, (7,))],
            [(1, range(1, 6)), (2, (6, 7)), (4, (0,))],
        ],
        [a2, b2, a3, b3, m4],
    )
    m5 = along_line(m4, up=range(4, 7), down=range(1, 4))
    m6 = along_line(m5, up=range(5, 7), down=range(1, 3))
    group(
        [
            [(0, range(1, 7)), (1, (0, 7))],
            [(1, (1, 2, 5, 6)), (2, (0, 7)), (3, (4,)), (4, (3,))],
        ],
        [m4, m5, m6, a3, b3],
    )
    m7 = along_line(m6, up=(6,), down=(1,))
    group(
        [[(0, (0, 7)), (1, (1, 6)), (2, (3, 5)), (3, (2, 4))]],
        [m7, m6, a3, b3],
    )
    last = along_x(left[-1][0:1], 1), along_x(right[-1][1:2], -1)
    return sent, left, right, last


def per_device(tokens, mix_weight, partner_offset, ln_gain, qkv_weight, qk_gain):
    x, zl, zh = lax.axis_index("x"), lax.axis_index("zl"), lax.axis_index("zh")

    partner_block = previous_images(tokens)
    lam = (mix_weight.astype(jnp.float32) / 256.0)[:, None, None]
    first = ((jnp.arange(2, dtype=jnp.int32) + partner_offset) % 2 == 0)[:, None, None]
    partner = jnp.where(first, partner_block[0], partner_block[1])
    mixed = lam * tokens.astype(jnp.float32) + (1.0 - lam) * partner.astype(jnp.float32)
    mixed = mixed.astype(jnp.bfloat16)

    ahead = along_z(along_z(mixed[0], 4), 4)
    behind = along_z(along_z(mixed[1], -4), -4)
    own_features = lax.all_gather(mixed.reshape(512, 384), ("y", "c"))
    other_features = lax.all_gather(jnp.concatenate([ahead, behind]), ("y", "c"))

    halves = jnp.stack([qkv_weight[:, :, :HEAD], qkv_weight[:, :, HEAD:]])
    sent, left, right, (last_left, last_right) = gather_weights(halves, zl)

    sources = jnp.asarray(SLOT_SOURCES)[zl]
    block_of = ((x + jnp.arange(4, dtype=jnp.int32)) % 4 * 8)[:, None] + sources[None, :]
    feature = block_of // 2
    index = block_of % 2 * 16 + (feature // 8 + zh) % 2 * 8 + feature % 8
    index = index.reshape(32).astype(jnp.int32)

    gain = ln_gain.reshape(2, 8, 384)
    gain = jnp.where(zh == 0, gain, gain[::-1]).reshape(16, 384)
    normed = norm_tokens(own_features, other_features, gain)

    def three(slot, place):
        return [
            (slot, ((0, 2 * place), (0, 2 * place + 1))),
            (8 + slot, ((2, 2 * place), (2, 2 * place + 1))),
            (24 + slot, ((1, 2 * place), (1, 2 * place + 1))),
        ]

    def at(blocks, base):
        return [
            (which, ((a[0] + base, a[1]), (b[0] + base, b[1]))) for which, (a, b) in blocks
        ]

    first_blocks, pieces = [], []
    for group, (slots_in, opposite) in enumerate(
        [((0,), ()), ((1, 2), (0,)), ((3, 4), (1, 2)), ((5, 6), (3, 4))]
    ):
        blocks = []
        for place, slot in enumerate(slots_in):
            blocks += three(slot, place)
        for place, slot in enumerate(opposite):
            tail = 2 * len(slots_in) + place
            blocks.append((16 + slot, ((1, tail), (2, tail))))
        first_blocks += at(blocks, 3 * group)
        pieces += [sent[group][0], left[group], right[group]]
    acc_shape = jax.ShapeDtypeStruct((3, 512, 256), jnp.float32)
    acc = project(first_kernel, first_blocks, index, normed, [], pieces, acc_shape)
    blocks = three(7, 0) + [(16 + 5, ((1, 2), (2, 2))), (16 + 6, ((1, 3), (2, 3)))]
    acc = project(
        next_kernel, blocks, index, normed, [acc], [sent[4][0], left[4], right[4]], acc_shape
    )
    out = project(
        last_kernel,
        [(16 + 7, ((0, 0), (1, 0)))],
        index,
        normed,
        [acc, qk_gain],
        [last_left, last_right],
        jax.ShapeDtypeStruct((512, 256), jnp.bfloat16),
        [pltpu.VMEM((3, 512, 256), jnp.float32)],
    )
    return out.reshape(2, 256, 256)


def solution(mesh):
    grid = Mesh(mesh.devices.reshape(SIZES), AXES)
    dp, tensor = ("x", "zl"), ("zh", "y", "c")
    placed = (
        P(dp, None, tensor),
        P(dp),
        P(dp),
        P(),
        P(None, dp, tensor),
        P(None, tensor),
    )
    return jax.shard_map(
        per_device, mesh=grid, in_specs=placed, out_specs=P(dp, None, tensor), check_vma=False
    )
```

```python
import functools

import jax
import jax.numpy as jnp
import numpy as np
from jax import lax
from jax.experimental import pallas as pl
from jax.experimental.pallas import tpu as pltpu
from jax.sharding import Mesh, PartitionSpec as P

HEAD = 128
AXES = ("x", "zl", "zh", "y", "c")
SIZES = (4, 8, 2, 4, 2)
VMEM_LIMIT = 32 * 1024 * 1024

SLOT_SOURCES = np.array(
    [
        [0, 2, 1, 3, 4, 5, 6, 7],
        [1, 0, 2, 4, 3, 5, 6, 7],
        [2, 1, 3, 0, 4, 6, 7, 5],
        [3, 2, 4, 1, 5, 7, 6, 0],
        [4, 3, 5, 2, 6, 0, 1, 7],
        [5, 4, 6, 3, 7, 1, 0, 2],
        [6, 5, 7, 4, 3, 2, 1, 0],
        [7, 6, 5, 3, 4, 2, 1, 0],
    ],
    dtype=np.int32,
)


def move(value, target):
    pairs = []
    for source in range(512):
        c = source % 2
        y = source // 2 % 4
        zh = source // 8 % 2
        zl = source // 16 % 8
        x = source // 128
        goal = target(x, zl, zh, y, c)
        if goal is None:
            continue
        gx, gzl, gzh, gy, gc = goal
        pairs.append((source, (((gx % 4 * 8 + gzl) * 2 + gzh) * 4 + gy % 4) * 2 + gc))
    return lax.ppermute(value, AXES, pairs)


def along_x(value, by):
    return move(value, lambda x, zl, zh, y, c: (x + by, zl, zh, y, c))


def along_z(value, by):
    def target(x, zl, zh, y, c):
        z = (zh * 8 + zl + by) % 16
        return x, z % 8, z // 8, y, c

    return move(value, target)


def along_line(value, up=(), down=()):
    def target(x, zl, zh, y, c):
        if zl in up:
            return x, zl + 1, zh, y, c
        if zl in down:
            return x, zl - 1, zh, y, c
        return None

    return move(value, target)


def previous_images(value):
    def target(x, zl, zh, y, c):
        dp = (x * 8 + zl - 1) % 32
        return dp // 8, dp % 8, zh, y, c

    return move(value, target)


def norm_last(values, eps):
    mean = jnp.mean(values, axis=-1, keepdims=True)
    centred = values - mean
    var = jnp.mean(centred * centred, axis=-1, keepdims=True)
    return centred / jnp.sqrt(var + eps)


def norm_kernel(own_ref, other_ref, gain_ref, out_ref):
    parts = [ref[j].astype(jnp.float32) for ref in (own_ref, other_ref) for j in range(8)]
    count = 16 * parts[0].shape[1]
    total = functools.reduce(jnp.add, parts)
    mean = jnp.sum(total, axis=-1, keepdims=True) / count
    parts = [part - mean for part in parts]
    total = functools.reduce(jnp.add, [part * part for part in parts])
    scale = 1.0 / jnp.sqrt(jnp.sum(total, axis=-1, keepdims=True) / count + 1e-06)
    for block, part in enumerate(parts):
        normed = (part * scale * gain_ref[block : block + 1, :]).astype(jnp.bfloat16)
        out_ref[block] = normed[:, :192]
        out_ref[16 + block] = normed[:, 192:]


def norm_tokens(own, other, gain):
    rows = 64
    return pl.pallas_call(
        norm_kernel,
        out_shape=jax.ShapeDtypeStruct((32, 512, 192), jnp.bfloat16),
        grid=(512 // rows,),
        in_specs=[
            pl.BlockSpec((8, rows, 384), lambda i: (0, i, 0)),
            pl.BlockSpec((8, rows, 384), lambda i: (0, i, 0)),
            pl.BlockSpec((16, 384), lambda i: (0, 0)),
        ],
        out_specs=pl.BlockSpec((32, rows, 192), lambda i: (0, i, 0)),
        compiler_params=pltpu.CompilerParams(vmem_limit_bytes=VMEM_LIMIT),
        cost_estimate=pl.CostEstimate(
            flops=512 * 6144 * 8, bytes_accessed=14 * 2**20, transcendentals=0
        ),
    )(own, other, gain)


def add_products(blocks, index_ref, normed_ref, piece_refs, acc_ref):
    for which, (left, right) in blocks:
        rows = normed_ref[index_ref[which]]
        for c in range(3):
            weight = jnp.concatenate(
                [piece_refs[left[0]][left[1], c], piece_refs[right[0]][right[1], c]], axis=-1
            )
            acc_ref[c] += jnp.dot(rows, weight, preferred_element_type=jnp.float32)


def first_kernel(blocks, index_ref, normed_ref, *refs):
    pieces, acc_ref = refs[:-1], refs[-1]
    acc_ref[...] = jnp.zeros_like(acc_ref)
    add_products(blocks, index_ref, normed_ref, pieces, acc_ref)


def next_kernel(blocks, index_ref, normed_ref, held_ref, *refs):
    pieces, acc_ref = refs[:-1], refs[-1]
    acc_ref[...] = held_ref[...]
    add_products(blocks, index_ref, normed_ref, pieces, acc_ref)


def attend(acc_ref, gain_ref, out_ref):
    for head in range(2):
        columns = slice(head * HEAD, (head + 1) * HEAD)
        for image in range(2):
            rows = slice(image * 256, (image + 1) * 256)
            query, keys, values = (
                acc_ref[c, rows, columns].astype(jnp.bfloat16) for c in range(3)
            )
            q_norm = (
                norm_last(query.astype(jnp.float32), 1e-06)
                * gain_ref[0:1, columns]
                * HEAD ** (-0.5)
            ).astype(jnp.bfloat16)
            k_norm = (
                norm_last(keys.astype(jnp.float32), 1e-06) * gain_ref[1:2, columns]
            ).astype(jnp.bfloat16)
            scores = lax.dot_general(
                q_norm, k_norm, (((1,), (1,)), ((), ())), preferred_element_type=jnp.float32
            )
            raised = jnp.exp(scores - jnp.max(scores, axis=-1, keepdims=True))
            probs = (raised / jnp.sum(raised, axis=-1, keepdims=True)).astype(jnp.bfloat16)
            out_ref[rows, columns] = jnp.dot(
                probs, values, preferred_element_type=jnp.float32
            ).astype(jnp.bfloat16)


def last_kernel(blocks, index_ref, normed_ref, held_ref, gain_ref, *refs):
    pieces, out_ref, acc_ref = refs[:-2], refs[-2], refs[-1]
    acc_ref[...] = held_ref[...]
    add_products(blocks, index_ref, normed_ref, pieces, acc_ref)
    attend(acc_ref, gain_ref, out_ref)


def project(kernel, blocks, index, normed, extra, pieces, out_shape, scratch=()):
    whole = pl.BlockSpec(memory_space=pltpu.VMEM)
    return pl.pallas_call(
        functools.partial(kernel, blocks),
        out_shape=out_shape,
        in_specs=[pl.BlockSpec(memory_space=pltpu.SMEM)] + [whole] * (1 + len(extra) + len(pieces)),
        out_specs=whole,
        scratch_shapes=list(scratch),
        compiler_params=pltpu.CompilerParams(vmem_limit_bytes=VMEM_LIMIT),
        cost_estimate=pl.CostEstimate(
            flops=len(blocks) * 512 * 192 * 768 * 2,
            bytes_accessed=8 * 2**20 + len(blocks) * 294912,
            transcendentals=0,
        ),
    )(index, normed, *extra, *pieces)


def relay_kernel(slots, forward, count, zl_ref, *refs):
    sources, rest = refs[:count], refs[count:]
    lefts, rest = rest[: len(forward)], rest[len(forward) :]
    rights, (to_right, to_left) = rest[: len(forward)], rest[-2:]
    zl = zl_ref[0]
    for place, choices in enumerate(slots):
        for source, rows in choices:
            chosen = functools.reduce(jnp.logical_or, [zl == row for row in rows])

            @pl.when(chosen)
            def _(source=source, place=place):
                block = sources[source][...]
                to_right[2 * place : 2 * place + 2] = block
                to_left[2 * place : 2 * place + 2] = block

    end = 2 * len(slots)
    for left_ref, right_ref, blocks in zip(lefts, rights, forward):
        for place in range(blocks):
            to_right[end] = left_ref[2 * place]
            to_left[end] = right_ref[2 * place + 1]
            end += 1


def relay(row, slots, arrays, lefts, rights, forward, after=()):
    whole = pl.BlockSpec(memory_space=pltpu.VMEM)
    message = jax.ShapeDtypeStruct((2 * len(slots) + sum(forward), 3, 192, HEAD), jnp.bfloat16)
    return pl.pallas_call(
        functools.partial(relay_kernel, slots, forward, len(arrays)),
        out_shape=(message, message),
        in_specs=[pl.BlockSpec(memory_space=pltpu.SMEM)]
        + [whole] * (len(arrays) + 2 * len(forward))
        + [pl.BlockSpec(memory_space=pl.ANY)] * len(after),
        out_specs=(whole, whole),
        compiler_params=pltpu.CompilerParams(vmem_limit_bytes=16 * 2**20),
        cost_estimate=pl.CostEstimate(flops=0, bytes_accessed=4 * 2**20, transcendentals=0),
    )(row, *arrays, *lefts, *rights, *after)


def mix_kernel(weight_ref, offset_ref, tokens_ref, partner_ref, *refs):
    mixed_ref = refs[-1]
    for image in range(2):
        lam = weight_ref[image].astype(jnp.float32) / 256.0
        partner = partner_ref[lax.rem(image + offset_ref[image], 2)]
        mixed = lam * tokens_ref[image].astype(jnp.float32) + (1.0 - lam) * partner.astype(
            jnp.float32
        )
        mixed_ref[image] = mixed.astype(jnp.bfloat16)


def mix(weight, offset, tokens, partner, after):
    whole, scalars = pl.BlockSpec(memory_space=pltpu.VMEM), pl.BlockSpec(memory_space=pltpu.SMEM)
    return pl.pallas_call(
        mix_kernel,
        out_shape=jax.ShapeDtypeStruct(tokens.shape, tokens.dtype),
        in_specs=[scalars, scalars, whole, whole]
        + [pl.BlockSpec(memory_space=pl.ANY)] * len(after),
        out_specs=whole,
        compiler_params=pltpu.CompilerParams(vmem_limit_bytes=8 * 2**20),
    )(weight, offset, tokens, partner, *after)


def copy_kernel(count, *refs):
    for source, target in zip(refs[:count], refs[-count:]):
        target[...] = source[...]


def held_back(values, after):
    whole = pl.BlockSpec(memory_space=pltpu.VMEM)
    return pl.pallas_call(
        functools.partial(copy_kernel, len(values)),
        out_shape=[jax.ShapeDtypeStruct(value.shape, value.dtype) for value in values],
        in_specs=[whole] * len(values) + [pl.BlockSpec(memory_space=pl.ANY)] * len(after),
        out_specs=[whole] * len(values),
        compiler_params=pltpu.CompilerParams(vmem_limit_bytes=8 * 2**20),
    )(*values, *after)


def other_kernel(zh_ref, first_ref, second_ref, *refs):
    refs[-1][0:256] = first_ref[...]
    refs[-1][256:512] = second_ref[1 - zh_ref[0]]


def other_half(zh, first_image, second_images, after):
    whole = pl.BlockSpec(memory_space=pltpu.VMEM)
    return pl.pallas_call(
        other_kernel,
        out_shape=jax.ShapeDtypeStruct((512, 384), jnp.bfloat16),
        in_specs=[pl.BlockSpec(memory_space=pltpu.SMEM), whole, whole]
        + [pl.BlockSpec(memory_space=pl.ANY)] * len(after),
        out_specs=whole,
        compiler_params=pltpu.CompilerParams(vmem_limit_bytes=8 * 2**20),
    )(zh, first_image, second_images, *after)


def either_kernel(zl_ref, upper_ref, lower_ref, *refs):
    @pl.when(zl_ref[0] >= 4)
    def _():
        refs[-1][...] = upper_ref[...]

    @pl.when(zl_ref[0] < 4)
    def _():
        refs[-1][...] = lower_ref[...]


def either(row, upper, lower, after):
    whole = pl.BlockSpec(memory_space=pltpu.VMEM)
    return pl.pallas_call(
        either_kernel,
        out_shape=jax.ShapeDtypeStruct(upper.shape, upper.dtype),
        in_specs=[pl.BlockSpec(memory_space=pltpu.SMEM), whole, whole]
        + [pl.BlockSpec(memory_space=pl.ANY)] * len(after),
        out_specs=whole,
        compiler_params=pltpu.CompilerParams(vmem_limit_bytes=8 * 2**20),
    )(row, upper, lower, *after)


def per_device(tokens, mix_weight, partner_offset, ln_gain, qkv_weight, qk_gain):
    x, zl, zh = lax.axis_index("x"), lax.axis_index("zl"), lax.axis_index("zh")

    halves = jnp.stack([qkv_weight[:, :, :HEAD], qkv_weight[:, :, HEAD:]])
    partner_block = previous_images(tokens)
    a1 = along_line(halves, up=range(0, 7))
    b1 = along_line(halves, down=range(1, 8))
    sent, left, right = [halves], [along_x(halves, 1)], [along_x(halves, -1)]

    mixed = mix(
        mix_weight, partner_offset, tokens, partner_block, [a1, b1, left[0], right[0]]
    )
    own_features = lax.all_gather(mixed.reshape(512, 384), ("y", "c"))
    second_images = lax.all_gather(mixed[1], "zh")
    first_image = along_z(mixed[0], 8)

    row = zl.reshape(1)

    def send(slots, arrays, forward, after=()):
        lefts = [left[group] for group, _ in forward]
        rights = [right[group] for group, _ in forward]
        to_right, to_left = relay(
            row, slots, arrays, lefts, rights, tuple(blocks for _, blocks in forward), after
        )
        sent.append(to_right)
        left.append(along_x(to_right, 1))
        right.append(along_x(to_left, -1))

    a2 = along_line(a1, up=range(1, 7))
    b2 = along_line(b1, down=range(1, 7))
    send(
        [[(0, range(1, 8)), (3, (0,))], [(1, range(0, 7)), (2, (7,))]],
        [a1, b1, a2, b2],
        [],
    )
    a3 = along_line(a2, up=range(2, 7))
    b3 = along_line(b2, down=range(1, 6))
    a4 = along_line(a3, up=range(3, 7))
    b4 = along_line(b3, down=range(1, 5))
    m4 = either(row, a4, b4, [left[1], right[1]])
    send(
        [
            [(0, range(2, 7)), (3, (0, 1)), (4, (7,))],
            [(1, range(1, 6)), (2, (6, 7)), (4, (0,))],
        ],
        [a2, b2, a3, b3, m4],
        [(0, 1)],
    )
    m5 = along_line(m4, up=range(4, 7), down=range(1, 4))
    m6 = along_line(m5, up=range(5, 7), down=range(1, 3))
    send(
        [
            [(0, range(1, 7)), (1, (0, 7))],
            [(1, (1, 2, 5, 6)), (2, (0, 7)), (3, (4,)), (4, (3,))],
        ],
        [m4, m5, m6, a3, b3],
        [(1, 2)],
    )
    other = other_half(zh.reshape(1), first_image, second_images, [m5])
    other_features = lax.all_gather(other, ("y", "c"))
    (held,) = held_back([m6], [left[2], right[2]])
    m7 = along_line(held, up=(6,), down=(1,))
    send(
        [[(0, (0, 7)), (1, (1, 6)), (2, (3, 5)), (3, (2, 4))]],
        [m7, m6, a3, b3],
        [(2, 2)],
    )

    sources = jnp.asarray(SLOT_SOURCES)[zl]
    block_of = ((x + jnp.arange(4, dtype=jnp.int32)) % 4 * 8)[:, None] + sources[None, :]
    feature = block_of // 2
    index = block_of % 2 * 16 + (feature // 8 + zh) % 2 * 8 + feature % 8
    index = index.reshape(32).astype(jnp.int32)

    gain = ln_gain.reshape(2, 8, 384)
    gain = jnp.where(zh == 0, gain, gain[::-1]).reshape(16, 384)
    normed = norm_tokens(own_features, other_features, gain)

    def three(slot, place):
        return [
            (slot, ((0, 2 * place), (0, 2 * place + 1))),
            (8 + slot, ((2, 2 * place), (2, 2 * place + 1))),
            (24 + slot, ((1, 2 * place), (1, 2 * place + 1))),
        ]

    def at(blocks, base):
        return [
            (which, ((a[0] + base, a[1]), (b[0] + base, b[1]))) for which, (a, b) in blocks
        ]

    def group_blocks(slots_in, opposite):
        blocks = []
        for place, slot in enumerate(slots_in):
            blocks += three(slot, place)
        for place, slot in enumerate(opposite):
            tail = 2 * len(slots_in) + place
            blocks.append((16 + slot, ((1, tail), (2, tail))))
        return blocks

    def arrays(group):
        return [sent[group], left[group], right[group]]

    first_blocks, pieces = [], []
    for group, (slots_in, opposite) in enumerate(
        [((0,), ()), ((1, 2), ()), ((3, 4), (0,)), ((5, 6), (1, 2))]
    ):
        first_blocks += at(group_blocks(slots_in, opposite), 3 * group)
        pieces += arrays(group)
    acc_shape = jax.ShapeDtypeStruct((3, 512, 256), jnp.float32)
    acc = project(first_kernel, first_blocks, index, normed, [], pieces, acc_shape)
    send([], [], [(3, 2), (4, 1)], [acc])
    acc = project(
        next_kernel, group_blocks((7,), (3, 4)), index, normed, [acc], arrays(4), acc_shape
    )
    out = project(
        last_kernel,
        at(group_blocks((), (5, 6, 7)), -1),
        index,
        normed,
        [acc, qk_gain],
        arrays(5)[1:],
        jax.ShapeDtypeStruct((512, 256), jnp.bfloat16),
        [pltpu.VMEM((3, 512, 256), jnp.float32)],
    )
    return out.reshape(2, 256, 256)


def solution(mesh):
    grid = Mesh(mesh.devices.reshape(SIZES), AXES)
    dp, tensor = ("x", "zl"), ("zh", "y", "c")
    placed = (
        P(dp, None, tensor),
        P(dp),
        P(dp),
        P(),
        P(None, dp, tensor),
        P(None, tensor),
    )
    return jax.shard_map(
        per_device, mesh=grid, in_specs=placed, out_specs=P(dp, None, tensor), check_vma=False
    )
```

```python
import functools

import jax
import jax.numpy as jnp
import numpy as np
from jax import lax
from jax.experimental import pallas as pl
from jax.experimental.pallas import tpu as pltpu
from jax.sharding import Mesh, PartitionSpec as P

HEAD = 128
AXES = ("x", "zl", "zh", "y", "c")
SIZES = (4, 8, 2, 4, 2)
VMEM_LIMIT = 32 * 1024 * 1024

SLOT_SOURCES = np.array(
    [
        [0, 2, 1, 3, 4, 5, 6, 7],
        [1, 0, 2, 4, 3, 5, 6, 7],
        [2, 1, 3, 0, 4, 6, 7, 5],
        [3, 2, 4, 1, 5, 7, 6, 0],
        [4, 3, 5, 2, 6, 0, 1, 7],
        [5, 4, 6, 3, 7, 1, 0, 2],
        [6, 5, 7, 4, 3, 2, 1, 0],
        [7, 6, 5, 3, 4, 2, 1, 0],
    ],
    dtype=np.int32,
)


def move(value, target):
    pairs = []
    for source in range(512):
        c = source % 2
        y = source // 2 % 4
        zh = source // 8 % 2
        zl = source // 16 % 8
        x = source // 128
        goal = target(x, zl, zh, y, c)
        if goal is None:
            continue
        gx, gzl, gzh, gy, gc = goal
        pairs.append((source, (((gx % 4 * 8 + gzl) * 2 + gzh) * 4 + gy % 4) * 2 + gc))
    return lax.ppermute(value, AXES, pairs)


def along_x(value, by):
    return move(value, lambda x, zl, zh, y, c: (x + by, zl, zh, y, c))


def along_z_both_ways(value):
    def target(x, zl, zh, y, c):
        z = zh * 8 + zl
        z = (z + 4 if z % 2 == 0 else z - 4) % 16
        return x, z % 8, z // 8, y, c

    return move(value, target)


def along_line(value, up=(), down=()):
    def target(x, zl, zh, y, c):
        if zl in up:
            return x, zl + 1, zh, y, c
        if zl in down:
            return x, zl - 1, zh, y, c
        return None

    return move(value, target)


def previous_images(value):
    def target(x, zl, zh, y, c):
        dp = (x * 8 + zl - 1) % 32
        return dp // 8, dp % 8, zh, y, c

    return move(value, target)


def norm_last(values, eps):
    mean = jnp.mean(values, axis=-1, keepdims=True)
    centred = values - mean
    var = jnp.mean(centred * centred, axis=-1, keepdims=True)
    return centred / jnp.sqrt(var + eps)


def norm_kernel(own_ref, other_ref, gain_ref, out_ref):
    parts = [ref[j].astype(jnp.float32) for ref in (own_ref, other_ref) for j in range(8)]
    count = 16 * parts[0].shape[1]
    total = functools.reduce(jnp.add, parts)
    mean = jnp.sum(total, axis=-1, keepdims=True) / count
    parts = [part - mean for part in parts]
    total = functools.reduce(jnp.add, [part * part for part in parts])
    scale = 1.0 / jnp.sqrt(jnp.sum(total, axis=-1, keepdims=True) / count + 1e-06)
    for block, part in enumerate(parts):
        normed = (part * scale * gain_ref[block : block + 1, :]).astype(jnp.bfloat16)
        out_ref[block] = normed[:, :192]
        out_ref[16 + block] = normed[:, 192:]


def norm_tokens(own, other, gain):
    rows = 64
    return pl.pallas_call(
        norm_kernel,
        out_shape=jax.ShapeDtypeStruct((32, 512, 192), jnp.bfloat16),
        grid=(512 // rows,),
        in_specs=[
            pl.BlockSpec((8, rows, 384), lambda i: (0, i, 0)),
            pl.BlockSpec((8, rows, 384), lambda i: (0, i, 0)),
            pl.BlockSpec((16, 384), lambda i: (0, 0)),
        ],
        out_specs=pl.BlockSpec((32, rows, 192), lambda i: (0, i, 0)),
        compiler_params=pltpu.CompilerParams(vmem_limit_bytes=VMEM_LIMIT),
        cost_estimate=pl.CostEstimate(
            flops=512 * 6144 * 8, bytes_accessed=14 * 2**20, transcendentals=0
        ),
    )(own, other, gain)


def add_products(blocks, index_ref, normed_ref, piece_refs, acc_ref):
    for which, (left, right) in blocks:
        rows = normed_ref[index_ref[which]]
        for c in range(3):
            weight = jnp.concatenate(
                [piece_refs[left[0]][left[1], c], piece_refs[right[0]][right[1], c]], axis=-1
            )
            acc_ref[c] += jnp.dot(rows, weight, preferred_element_type=jnp.float32)


def first_kernel(blocks, index_ref, normed_ref, *refs):
    pieces, acc_ref = refs[:-1], refs[-1]
    acc_ref[...] = jnp.zeros_like(acc_ref)
    add_products(blocks, index_ref, normed_ref, pieces, acc_ref)


def next_kernel(blocks, index_ref, normed_ref, held_ref, *refs):
    pieces, acc_ref = refs[:-1], refs[-1]
    acc_ref[...] = held_ref[...]
    add_products(blocks, index_ref, normed_ref, pieces, acc_ref)


def attend(acc_ref, gain_ref, out_ref):
    for head in range(2):
        columns = slice(head * HEAD, (head + 1) * HEAD)
        for image in range(2):
            rows = slice(image * 256, (image + 1) * 256)
            query, keys, values = (
                acc_ref[c, rows, columns].astype(jnp.bfloat16) for c in range(3)
            )
            q_norm = (
                norm_last(query.astype(jnp.float32), 1e-06)
                * gain_ref[0:1, columns]
                * HEAD ** (-0.5)
            ).astype(jnp.bfloat16)
            k_norm = (
                norm_last(keys.astype(jnp.float32), 1e-06) * gain_ref[1:2, columns]
            ).astype(jnp.bfloat16)
            scores = lax.dot_general(
                q_norm, k_norm, (((1,), (1,)), ((), ())), preferred_element_type=jnp.float32
            )
            raised = jnp.exp(scores - jnp.max(scores, axis=-1, keepdims=True))
            probs = (raised / jnp.sum(raised, axis=-1, keepdims=True)).astype(jnp.bfloat16)
            out_ref[rows, columns] = jnp.dot(
                probs, values, preferred_element_type=jnp.float32
            ).astype(jnp.bfloat16)


def last_kernel(blocks, index_ref, normed_ref, held_ref, gain_ref, *refs):
    pieces, out_ref, acc_ref = refs[:-2], refs[-2], refs[-1]
    acc_ref[...] = held_ref[...]
    add_products(blocks, index_ref, normed_ref, pieces, acc_ref)
    attend(acc_ref, gain_ref, out_ref)


def project(kernel, blocks, index, normed, extra, pieces, out_shape, scratch=()):
    whole = pl.BlockSpec(memory_space=pltpu.VMEM)
    return pl.pallas_call(
        functools.partial(kernel, blocks),
        out_shape=out_shape,
        in_specs=[pl.BlockSpec(memory_space=pltpu.SMEM)] + [whole] * (1 + len(extra) + len(pieces)),
        out_specs=whole,
        scratch_shapes=list(scratch),
        compiler_params=pltpu.CompilerParams(vmem_limit_bytes=VMEM_LIMIT),
        cost_estimate=pl.CostEstimate(
            flops=len(blocks) * 512 * 192 * 768 * 2,
            bytes_accessed=8 * 2**20 + len(blocks) * 294912,
            transcendentals=0,
        ),
    )(index, normed, *extra, *pieces)


def relay_kernel(slots, forward, count, zl_ref, *refs):
    sources, rest = refs[:count], refs[count:]
    lefts, rest = rest[: len(forward)], rest[len(forward) :]
    rights, (to_right, to_left) = rest[: len(forward)], rest[-2:]
    zl = zl_ref[0]
    for place, choices in enumerate(slots):
        for source, rows in choices:
            chosen = functools.reduce(jnp.logical_or, [zl == row for row in rows])

            @pl.when(chosen)
            def _(source=source, place=place):
                block = sources[source][...]
                to_right[2 * place : 2 * place + 2] = block
                to_left[2 * place : 2 * place + 2] = block

    end = 2 * len(slots)
    for left_ref, right_ref, blocks in zip(lefts, rights, forward):
        for place in range(blocks):
            to_right[end] = left_ref[2 * place]
            to_left[end] = right_ref[2 * place + 1]
            end += 1


def relay(row, slots, arrays, lefts, rights, forward, after=()):
    whole = pl.BlockSpec(memory_space=pltpu.VMEM)
    message = jax.ShapeDtypeStruct((2 * len(slots) + sum(forward), 3, 192, HEAD), jnp.bfloat16)
    return pl.pallas_call(
        functools.partial(relay_kernel, slots, forward, len(arrays)),
        out_shape=(message, message),
        in_specs=[pl.BlockSpec(memory_space=pltpu.SMEM)]
        + [whole] * (len(arrays) + 2 * len(forward))
        + [pl.BlockSpec(memory_space=pl.ANY)] * len(after),
        out_specs=(whole, whole),
        compiler_params=pltpu.CompilerParams(vmem_limit_bytes=16 * 2**20),
        cost_estimate=pl.CostEstimate(flops=0, bytes_accessed=4 * 2**20, transcendentals=0),
    )(row, *arrays, *lefts, *rights, *after)


def mix_kernel(weight_ref, offset_ref, tokens_ref, partner_ref, *refs):
    mixed_ref = refs[-1]
    for image in range(2):
        lam = weight_ref[image].astype(jnp.float32) / 256.0
        partner = partner_ref[lax.rem(image + offset_ref[image], 2)]
        mixed = lam * tokens_ref[image].astype(jnp.float32) + (1.0 - lam) * partner.astype(
            jnp.float32
        )
        mixed_ref[image] = mixed.astype(jnp.bfloat16)


def mix(weight, offset, tokens, partner, after):
    whole, scalars = pl.BlockSpec(memory_space=pltpu.VMEM), pl.BlockSpec(memory_space=pltpu.SMEM)
    return pl.pallas_call(
        mix_kernel,
        out_shape=jax.ShapeDtypeStruct(tokens.shape, tokens.dtype),
        in_specs=[scalars, scalars, whole, whole]
        + [pl.BlockSpec(memory_space=pl.ANY)] * len(after),
        out_specs=whole,
        compiler_params=pltpu.CompilerParams(vmem_limit_bytes=8 * 2**20),
    )(weight, offset, tokens, partner, *after)


def copy_kernel(count, *refs):
    for source, target in zip(refs[:count], refs[-count:]):
        target[...] = source[...]


def held_back(values, after):
    whole = pl.BlockSpec(memory_space=pltpu.VMEM)
    return pl.pallas_call(
        functools.partial(copy_kernel, len(values)),
        out_shape=[jax.ShapeDtypeStruct(value.shape, value.dtype) for value in values],
        in_specs=[whole] * len(values) + [pl.BlockSpec(memory_space=pl.ANY)] * len(after),
        out_specs=[whole] * len(values),
        compiler_params=pltpu.CompilerParams(vmem_limit_bytes=8 * 2**20),
    )(*values, *after)


def either_kernel(zl_ref, upper_ref, lower_ref, *refs):
    @pl.when(zl_ref[0] >= 4)
    def _():
        refs[-1][...] = upper_ref[...]

    @pl.when(zl_ref[0] < 4)
    def _():
        refs[-1][...] = lower_ref[...]


def either(row, upper, lower, after):
    whole = pl.BlockSpec(memory_space=pltpu.VMEM)
    return pl.pallas_call(
        either_kernel,
        out_shape=jax.ShapeDtypeStruct(upper.shape, upper.dtype),
        in_specs=[pl.BlockSpec(memory_space=pltpu.SMEM), whole, whole]
        + [pl.BlockSpec(memory_space=pl.ANY)] * len(after),
        out_specs=whole,
        compiler_params=pltpu.CompilerParams(vmem_limit_bytes=8 * 2**20),
    )(row, upper, lower, *after)


def per_device(tokens, mix_weight, partner_offset, ln_gain, qkv_weight, qk_gain):
    x, zl, zh = lax.axis_index("x"), lax.axis_index("zl"), lax.axis_index("zh")

    halves = jnp.stack([qkv_weight[:, :, :HEAD], qkv_weight[:, :, HEAD:]])
    partner_block = previous_images(tokens)
    a1 = along_line(halves, up=range(0, 7))
    b1 = along_line(halves, down=range(1, 8))
    sent, left, right = [halves], [along_x(halves, 1)], [along_x(halves, -1)]

    mixed = mix(
        mix_weight, partner_offset, tokens, partner_block, [a1, b1, left[0], right[0]]
    )
    own_features = lax.all_gather(mixed.reshape(512, 384), ("y", "c"))
    halfway = along_z_both_ways(mixed.reshape(512, 384))

    row = zl.reshape(1)

    def send(slots, arrays, forward, after=()):
        lefts = [left[group] for group, _ in forward]
        rights = [right[group] for group, _ in forward]
        to_right, to_left = relay(
            row, slots, arrays, lefts, rights, tuple(blocks for _, blocks in forward), after
        )
        sent.append(to_right)
        left.append(along_x(to_right, 1))
        right.append(along_x(to_left, -1))

    a2 = along_line(a1, up=range(1, 7))
    b2 = along_line(b1, down=range(1, 7))
    send(
        [[(0, range(1, 8)), (3, (0,))], [(1, range(0, 7)), (2, (7,))]],
        [a1, b1, a2, b2],
        [],
    )
    a3 = along_line(a2, up=range(2, 7))
    b3 = along_line(b2, down=range(1, 6))
    (halfway,) = held_back([halfway], [a3, b3])
    other = along_z_both_ways(halfway)
    a4 = along_line(a3, up=range(3, 7))
    b4 = along_line(b3, down=range(1, 5))
    m4 = either(row, a4, b4, [left[1], right[1]])
    send(
        [
            [(0, range(2, 7)), (3, (0, 1)), (4, (7,))],
            [(1, range(1, 6)), (2, (6, 7)), (4, (0,))],
        ],
        [a2, b2, a3, b3, m4],
        [(0, 1)],
    )
    m5 = along_line(m4, up=range(4, 7), down=range(1, 4))
    (other,) = held_back([other], [m5])
    other_features = lax.all_gather(other, ("y", "c"))
    m6 = along_line(m5, up=range(5, 7), down=range(1, 3))
    send(
        [
            [(0, range(1, 7)), (1, (0, 7))],
            [(1, (1, 2, 5, 6)), (2, (0, 7)), (3, (4,)), (4, (3,))],
        ],
        [m4, m5, m6, a3, b3],
        [(1, 2)],
    )
    m7 = along_line(m6, up=(6,), down=(1,))
    send(
        [[(0, (0, 7)), (1, (1, 6)), (2, (3, 5)), (3, (2, 4))]],
        [m7, m6, a3, b3],
        [(2, 2)],
    )

    sources = jnp.asarray(SLOT_SOURCES)[zl]
    block_of = ((x + jnp.arange(4, dtype=jnp.int32)) % 4 * 8)[:, None] + sources[None, :]
    feature = block_of // 2
    index = block_of % 2 * 16 + (feature // 8 + zh) % 2 * 8 + feature % 8
    index = index.reshape(32).astype(jnp.int32)

    gain = ln_gain.reshape(2, 8, 384)
    gain = jnp.where(zh == 0, gain, gain[::-1]).reshape(16, 384)
    normed = norm_tokens(own_features, other_features, gain)

    def three(slot, place):
        return [
            (slot, ((0, 2 * place), (0, 2 * place + 1))),
            (8 + slot, ((2, 2 * place), (2, 2 * place + 1))),
            (24 + slot, ((1, 2 * place), (1, 2 * place + 1))),
        ]

    def at(blocks, base):
        return [
            (which, ((a[0] + base, a[1]), (b[0] + base, b[1]))) for which, (a, b) in blocks
        ]

    def group_blocks(slots_in, opposite):
        blocks = []
        for place, slot in enumerate(slots_in):
            blocks += three(slot, place)
        for place, slot in enumerate(opposite):
            tail = 2 * len(slots_in) + place
            blocks.append((16 + slot, ((1, tail), (2, tail))))
        return blocks

    def arrays(group):
        return [sent[group], left[group], right[group]]

    first_blocks, pieces = [], []
    for group, (slots_in, opposite) in enumerate(
        [((0,), ()), ((1, 2), ()), ((3, 4), (0,)), ((5, 6), (1, 2))]
    ):
        first_blocks += at(group_blocks(slots_in, opposite), 3 * group)
        pieces += arrays(group)
    acc_shape = jax.ShapeDtypeStruct((3, 512, 256), jnp.float32)
    acc = project(first_kernel, first_blocks, index, normed, [], pieces, acc_shape)
    send([], [], [(3, 2), (4, 1)], [acc])
    acc = project(
        next_kernel, group_blocks((7,), (3, 4)), index, normed, [acc], arrays(4), acc_shape
    )
    out = project(
        last_kernel,
        at(group_blocks((), (5, 6, 7)), -1),
        index,
        normed,
        [acc, qk_gain],
        arrays(5)[1:],
        jax.ShapeDtypeStruct((512, 256), jnp.bfloat16),
        [pltpu.VMEM((3, 512, 256), jnp.float32)],
    )
    return out.reshape(2, 256, 256)


def solution(mesh):
    grid = Mesh(mesh.devices.reshape(SIZES), AXES)
    dp, tensor = ("x", "zl"), ("zh", "y", "c")
    placed = (
        P(dp, None, tensor),
        P(dp),
        P(dp),
        P(),
        P(None, dp, tensor),
        P(None, tensor),
    )
    return jax.shard_map(
        per_device, mesh=grid, in_specs=placed, out_specs=P(dp, None, tensor), check_vma=False
    )
```

```python
import functools

import jax
import jax.numpy as jnp
import numpy as np
from jax import lax
from jax.experimental import pallas as pl
from jax.experimental.pallas import tpu as pltpu
from jax.sharding import Mesh, PartitionSpec as P

HEAD = 128
AXES = ("x", "zl", "zh", "y", "c")
SIZES = (4, 8, 2, 4, 2)
VMEM_LIMIT = 32 * 1024 * 1024

SLOT_SOURCES = np.array(
    [
        [0, 2, 1, 3, 4, 5, 6, 7],
        [1, 0, 2, 4, 3, 5, 6, 7],
        [2, 1, 3, 0, 4, 6, 7, 5],
        [3, 2, 4, 1, 5, 7, 6, 0],
        [4, 3, 5, 2, 6, 0, 1, 7],
        [5, 4, 6, 3, 7, 1, 0, 2],
        [6, 5, 7, 4, 3, 2, 1, 0],
        [7, 6, 5, 3, 4, 2, 1, 0],
    ],
    dtype=np.int32,
)


def move(value, target):
    pairs = []
    for source in range(512):
        c = source % 2
        y = source // 2 % 4
        zh = source // 8 % 2
        zl = source // 16 % 8
        x = source // 128
        goal = target(x, zl, zh, y, c)
        if goal is None:
            continue
        gx, gzl, gzh, gy, gc = goal
        pairs.append((source, (((gx % 4 * 8 + gzl) * 2 + gzh) * 4 + gy % 4) * 2 + gc))
    return lax.ppermute(value, AXES, pairs)


def along_x(value, by):
    return move(value, lambda x, zl, zh, y, c: (x + by, zl, zh, y, c))


def along_z_both_ways(value):
    def target(x, zl, zh, y, c):
        z = zh * 8 + zl
        z = (z + 4 if z % 2 == 0 else z - 4) % 16
        return x, z % 8, z // 8, y, c

    return move(value, target)


def along_line(value, up=(), down=()):
    def target(x, zl, zh, y, c):
        if zl in up:
            return x, zl + 1, zh, y, c
        if zl in down:
            return x, zl - 1, zh, y, c
        return None

    return move(value, target)


def previous_images(value):
    def target(x, zl, zh, y, c):
        dp = (x * 8 + zl - 1) % 32
        return dp // 8, dp % 8, zh, y, c

    return move(value, target)


def norm_last(values, eps):
    mean = jnp.mean(values, axis=-1, keepdims=True)
    centred = values - mean
    var = jnp.mean(centred * centred, axis=-1, keepdims=True)
    return centred / jnp.sqrt(var + eps)


def norm_kernel(own_ref, other_ref, gain_ref, out_ref):
    parts = [ref[j].astype(jnp.float32) for ref in (own_ref, other_ref) for j in range(8)]
    count = 16 * parts[0].shape[1]
    total = functools.reduce(jnp.add, parts)
    mean = jnp.sum(total, axis=-1, keepdims=True) / count
    parts = [part - mean for part in parts]
    total = functools.reduce(jnp.add, [part * part for part in parts])
    scale = 1.0 / jnp.sqrt(jnp.sum(total, axis=-1, keepdims=True) / count + 1e-06)
    for block, part in enumerate(parts):
        normed = (part * scale * gain_ref[block : block + 1, :]).astype(jnp.bfloat16)
        out_ref[block] = normed[:, :192]
        out_ref[16 + block] = normed[:, 192:]


def norm_tokens(own, other, gain):
    rows = 64
    return pl.pallas_call(
        norm_kernel,
        out_shape=jax.ShapeDtypeStruct((32, 512, 192), jnp.bfloat16),
        grid=(512 // rows,),
        in_specs=[
            pl.BlockSpec((8, rows, 384), lambda i: (0, i, 0)),
            pl.BlockSpec((8, rows, 384), lambda i: (0, i, 0)),
            pl.BlockSpec((16, 384), lambda i: (0, 0)),
        ],
        out_specs=pl.BlockSpec((32, rows, 192), lambda i: (0, i, 0)),
        compiler_params=pltpu.CompilerParams(vmem_limit_bytes=VMEM_LIMIT),
        cost_estimate=pl.CostEstimate(
            flops=512 * 6144 * 8, bytes_accessed=14 * 2**20, transcendentals=0
        ),
    )(own, other, gain)


def add_products(blocks, index_ref, normed_ref, piece_refs, acc_ref):
    for which, (left, right) in blocks:
        rows = normed_ref[index_ref[which]]
        for c in range(3):
            weight = jnp.concatenate(
                [piece_refs[left[0]][left[1], c], piece_refs[right[0]][right[1], c]], axis=-1
            )
            acc_ref[c] += jnp.dot(rows, weight, preferred_element_type=jnp.float32)


def first_kernel(blocks, index_ref, normed_ref, *refs):
    pieces, acc_ref = refs[:-1], refs[-1]
    acc_ref[...] = jnp.zeros_like(acc_ref)
    add_products(blocks, index_ref, normed_ref, pieces, acc_ref)


def next_kernel(blocks, index_ref, normed_ref, held_ref, *refs):
    pieces, acc_ref = refs[:-1], refs[-1]
    acc_ref[...] = held_ref[...]
    add_products(blocks, index_ref, normed_ref, pieces, acc_ref)


def attend(acc_ref, gain_ref, out_ref):
    for head in range(2):
        columns = slice(head * HEAD, (head + 1) * HEAD)
        for image in range(2):
            rows = slice(image * 256, (image + 1) * 256)
            query, keys, values = (
                acc_ref[c, rows, columns].astype(jnp.bfloat16) for c in range(3)
            )
            q_norm = (
                norm_last(query.astype(jnp.float32), 1e-06)
                * gain_ref[0:1, columns]
                * HEAD ** (-0.5)
            ).astype(jnp.bfloat16)
            k_norm = (
                norm_last(keys.astype(jnp.float32), 1e-06) * gain_ref[1:2, columns]
            ).astype(jnp.bfloat16)
            scores = lax.dot_general(
                q_norm, k_norm, (((1,), (1,)), ((), ())), preferred_element_type=jnp.float32
            )
            raised = jnp.exp(scores - jnp.max(scores, axis=-1, keepdims=True))
            probs = (raised / jnp.sum(raised, axis=-1, keepdims=True)).astype(jnp.bfloat16)
            out_ref[rows, columns] = jnp.dot(
                probs, values, preferred_element_type=jnp.float32
            ).astype(jnp.bfloat16)


def last_kernel(blocks, index_ref, normed_ref, held_ref, gain_ref, *refs):
    pieces, out_ref, acc_ref = refs[:-2], refs[-2], refs[-1]
    acc_ref[...] = held_ref[...]
    add_products(blocks, index_ref, normed_ref, pieces, acc_ref)
    attend(acc_ref, gain_ref, out_ref)


def project(kernel, blocks, index, normed, extra, pieces, out_shape, scratch=()):
    whole = pl.BlockSpec(memory_space=pltpu.VMEM)
    return pl.pallas_call(
        functools.partial(kernel, blocks),
        out_shape=out_shape,
        in_specs=[pl.BlockSpec(memory_space=pltpu.SMEM)] + [whole] * (1 + len(extra) + len(pieces)),
        out_specs=whole,
        scratch_shapes=list(scratch),
        compiler_params=pltpu.CompilerParams(vmem_limit_bytes=VMEM_LIMIT),
        cost_estimate=pl.CostEstimate(
            flops=len(blocks) * 512 * 192 * 768 * 2,
            bytes_accessed=8 * 2**20 + len(blocks) * 294912,
            transcendentals=0,
        ),
    )(index, normed, *extra, *pieces)


def relay_kernel(slots, forward, count, zl_ref, *refs):
    sources, rest = refs[:count], refs[count:]
    lefts, rest = rest[: len(forward)], rest[len(forward) :]
    rights, (to_right, to_left) = rest[: len(forward)], rest[-2:]
    zl = zl_ref[0]
    for place, choices in enumerate(slots):
        for source, rows in choices:
            chosen = functools.reduce(jnp.logical_or, [zl == row for row in rows])

            @pl.when(chosen)
            def _(source=source, place=place):
                block = sources[source][...]
                to_right[2 * place : 2 * place + 2] = block
                to_left[2 * place : 2 * place + 2] = block

    end = 2 * len(slots)
    for left_ref, right_ref, blocks in zip(lefts, rights, forward):
        for place in range(blocks):
            to_right[end] = left_ref[2 * place]
            to_left[end] = right_ref[2 * place + 1]
            end += 1


def relay(row, slots, arrays, lefts, rights, forward, after=()):
    whole = pl.BlockSpec(memory_space=pltpu.VMEM)
    message = jax.ShapeDtypeStruct((2 * len(slots) + sum(forward), 3, 192, HEAD), jnp.bfloat16)
    return pl.pallas_call(
        functools.partial(relay_kernel, slots, forward, len(arrays)),
        out_shape=(message, message),
        in_specs=[pl.BlockSpec(memory_space=pltpu.SMEM)]
        + [whole] * (len(arrays) + 2 * len(forward))
        + [pl.BlockSpec(memory_space=pl.ANY)] * len(after),
        out_specs=(whole, whole),
        compiler_params=pltpu.CompilerParams(vmem_limit_bytes=16 * 2**20),
        cost_estimate=pl.CostEstimate(flops=0, bytes_accessed=4 * 2**20, transcendentals=0),
    )(row, *arrays, *lefts, *rights, *after)


def mix_kernel(weight_ref, offset_ref, tokens_ref, partner_ref, *refs):
    mixed_ref = refs[-1]
    for image in range(2):
        lam = weight_ref[image].astype(jnp.float32) / 256.0
        partner = partner_ref[lax.rem(image + offset_ref[image], 2)]
        mixed = lam * tokens_ref[image].astype(jnp.float32) + (1.0 - lam) * partner.astype(
            jnp.float32
        )
        mixed_ref[image] = mixed.astype(jnp.bfloat16)


def mix(weight, offset, tokens, partner, after):
    whole, scalars = pl.BlockSpec(memory_space=pltpu.VMEM), pl.BlockSpec(memory_space=pltpu.SMEM)
    return pl.pallas_call(
        mix_kernel,
        out_shape=jax.ShapeDtypeStruct(tokens.shape, tokens.dtype),
        in_specs=[scalars, scalars, whole, whole]
        + [pl.BlockSpec(memory_space=pl.ANY)] * len(after),
        out_specs=whole,
        compiler_params=pltpu.CompilerParams(vmem_limit_bytes=8 * 2**20),
    )(weight, offset, tokens, partner, *after)


def copy_kernel(count, *refs):
    for source, target in zip(refs[:count], refs[-count:]):
        target[...] = source[...]


def held_back(values, after):
    whole = pl.BlockSpec(memory_space=pltpu.VMEM)
    return pl.pallas_call(
        functools.partial(copy_kernel, len(values)),
        out_shape=[jax.ShapeDtypeStruct(value.shape, value.dtype) for value in values],
        in_specs=[whole] * len(values) + [pl.BlockSpec(memory_space=pl.ANY)] * len(after),
        out_specs=[whole] * len(values),
        compiler_params=pltpu.CompilerParams(vmem_limit_bytes=8 * 2**20),
    )(*values, *after)


def either_kernel(zl_ref, upper_ref, lower_ref, *refs):
    @pl.when(zl_ref[0] >= 4)
    def _():
        refs[-1][...] = upper_ref[...]

    @pl.when(zl_ref[0] < 4)
    def _():
        refs[-1][...] = lower_ref[...]


def either(row, upper, lower, after):
    whole = pl.BlockSpec(memory_space=pltpu.VMEM)
    return pl.pallas_call(
        either_kernel,
        out_shape=jax.ShapeDtypeStruct(upper.shape, upper.dtype),
        in_specs=[pl.BlockSpec(memory_space=pltpu.SMEM), whole, whole]
        + [pl.BlockSpec(memory_space=pl.ANY)] * len(after),
        out_specs=whole,
        compiler_params=pltpu.CompilerParams(vmem_limit_bytes=8 * 2**20),
    )(row, upper, lower, *after)


def per_device(tokens, mix_weight, partner_offset, ln_gain, qkv_weight, qk_gain):
    x, zl, zh = lax.axis_index("x"), lax.axis_index("zl"), lax.axis_index("zh")

    halves = jnp.stack([qkv_weight[:, :, :HEAD], qkv_weight[:, :, HEAD:]])
    partner_block = previous_images(tokens)
    a1 = along_line(halves, up=range(0, 7))
    b1 = along_line(halves, down=range(1, 8))
    sent, left, right = [halves], [along_x(halves, 1)], [along_x(halves, -1)]

    mixed = mix(
        mix_weight, partner_offset, tokens, partner_block, [a1, b1, left[0], right[0]]
    )
    own_features = lax.all_gather(mixed.reshape(512, 384), ("y", "c"))
    halfway = along_z_both_ways(mixed.reshape(512, 384))

    row = zl.reshape(1)

    def send(slots, arrays, forward, after=()):
        lefts = [left[group] for group, _ in forward]
        rights = [right[group] for group, _ in forward]
        to_right, to_left = relay(
            row, slots, arrays, lefts, rights, tuple(blocks for _, blocks in forward), after
        )
        sent.append(to_right)
        left.append(along_x(to_right, 1))
        right.append(along_x(to_left, -1))

    a2 = along_line(a1, up=range(1, 7))
    b2 = along_line(b1, down=range(1, 7))
    send(
        [[(0, range(1, 8)), (3, (0,))], [(1, range(0, 7)), (2, (7,))]],
        [a1, b1, a2, b2],
        [],
    )
    a3 = along_line(a2, up=range(2, 7))
    b3 = along_line(b2, down=range(1, 6))
    (halfway,) = held_back([halfway], [a3, b3])
    other = along_z_both_ways(halfway)
    a4 = along_line(a3, up=range(3, 7))
    b4 = along_line(b3, down=range(1, 5))
    m4 = either(row, a4, b4, [left[1], right[1]])
    send(
        [
            [(0, range(2, 7)), (3, (0, 1)), (4, (7,))],
            [(1, range(1, 6)), (2, (6, 7)), (4, (0,))],
        ],
        [a2, b2, a3, b3, m4],
        [(0, 1)],
    )
    m5 = along_line(m4, up=range(4, 7), down=range(1, 4))
    (other,) = held_back([other], [m5, sent[2]])
    other_features = lax.all_gather(other, ("y", "c"))
    m6 = along_line(m5, up=range(5, 7), down=range(1, 3))
    send(
        [
            [(0, range(1, 7)), (1, (0, 7))],
            [(1, (1, 2, 5, 6)), (2, (0, 7)), (3, (4,)), (4, (3,))],
        ],
        [m4, m5, m6, a3, b3],
        [(1, 2)],
    )
    m7 = along_line(m6, up=(6,), down=(1,))
    send(
        [[(0, (0, 7)), (1, (1, 6)), (2, (3, 5)), (3, (2, 4))]],
        [m7, m6, a3, b3],
        [(2, 2)],
    )

    sources = jnp.asarray(SLOT_SOURCES)[zl]
    block_of = ((x + jnp.arange(4, dtype=jnp.int32)) % 4 * 8)[:, None] + sources[None, :]
    feature = block_of // 2
    index = block_of % 2 * 16 + (feature // 8 + zh) % 2 * 8 + feature % 8
    index = index.reshape(32).astype(jnp.int32)

    gain = ln_gain.reshape(2, 8, 384)
    gain = jnp.where(zh == 0, gain, gain[::-1]).reshape(16, 384)
    normed = norm_tokens(own_features, other_features, gain)

    def three(slot, place):
        return [
            (slot, ((0, 2 * place), (0, 2 * place + 1))),
            (8 + slot, ((2, 2 * place), (2, 2 * place + 1))),
            (24 + slot, ((1, 2 * place), (1, 2 * place + 1))),
        ]

    def at(blocks, base):
        return [
            (which, ((a[0] + base, a[1]), (b[0] + base, b[1]))) for which, (a, b) in blocks
        ]

    def group_blocks(slots_in, opposite):
        blocks = []
        for place, slot in enumerate(slots_in):
            blocks += three(slot, place)
        for place, slot in enumerate(opposite):
            tail = 2 * len(slots_in) + place
            blocks.append((16 + slot, ((1, tail), (2, tail))))
        return blocks

    def arrays(group):
        return [sent[group], left[group], right[group]]

    first_blocks, pieces = [], []
    for group, (slots_in, opposite) in enumerate(
        [((0,), ()), ((1, 2), ()), ((3, 4), (0,)), ((5, 6), (1, 2))]
    ):
        first_blocks += at(group_blocks(slots_in, opposite), 3 * group)
        pieces += arrays(group)
    acc_shape = jax.ShapeDtypeStruct((3, 512, 256), jnp.float32)
    acc = project(first_kernel, first_blocks, index, normed, [], pieces, acc_shape)
    send([], [], [(3, 2), (4, 1)], [acc])
    acc = project(
        next_kernel, group_blocks((7,), (3, 4)), index, normed, [acc], arrays(4), acc_shape
    )
    out = project(
        last_kernel,
        at(group_blocks((), (5, 6, 7)), -1),
        index,
        normed,
        [acc, qk_gain],
        arrays(5)[1:],
        jax.ShapeDtypeStruct((512, 256), jnp.bfloat16),
        [pltpu.VMEM((3, 512, 256), jnp.float32)],
    )
    return out.reshape(2, 256, 256)


def solution(mesh):
    grid = Mesh(mesh.devices.reshape(SIZES), AXES)
    dp, tensor = ("x", "zl"), ("zh", "y", "c")
    placed = (
        P(dp, None, tensor),
        P(dp),
        P(dp),
        P(),
        P(None, dp, tensor),
        P(None, tensor),
    )
    return jax.shard_map(
        per_device, mesh=grid, in_specs=placed, out_specs=P(dp, None, tensor), check_vma=False
    )
```

```python
import functools

import jax
import jax.numpy as jnp
import numpy as np
from jax import lax
from jax.experimental import pallas as pl
from jax.experimental.pallas import tpu as pltpu
from jax.sharding import Mesh, PartitionSpec as P

HEAD = 128
AXES = ("x", "zl", "zh", "y", "c")
SIZES = (4, 8, 2, 4, 2)
VMEM_LIMIT = 32 * 1024 * 1024

SLOT_SOURCES = np.array(
    [
        [0, 2, 1, 3, 4, 5, 6, 7],
        [1, 0, 2, 4, 3, 5, 6, 7],
        [2, 1, 3, 0, 4, 6, 7, 5],
        [3, 2, 4, 1, 5, 7, 6, 0],
        [4, 3, 5, 2, 6, 0, 1, 7],
        [5, 4, 6, 3, 7, 1, 0, 2],
        [6, 5, 7, 4, 3, 2, 1, 0],
        [7, 6, 5, 3, 4, 2, 1, 0],
    ],
    dtype=np.int32,
)


def move(value, target):
    pairs = []
    for source in range(512):
        c = source % 2
        y = source // 2 % 4
        zh = source // 8 % 2
        zl = source // 16 % 8
        x = source // 128
        goal = target(x, zl, zh, y, c)
        if goal is None:
            continue
        gx, gzl, gzh, gy, gc = goal
        pairs.append((source, (((gx % 4 * 8 + gzl) * 2 + gzh) * 4 + gy % 4) * 2 + gc))
    return lax.ppermute(value, AXES, pairs)


def along_x(value, by):
    return move(value, lambda x, zl, zh, y, c: (x + by, zl, zh, y, c))


def along_z_both_ways(value):
    def target(x, zl, zh, y, c):
        z = zh * 8 + zl
        z = (z + 4 if z % 2 == 0 else z - 4) % 16
        return x, z % 8, z // 8, y, c

    return move(value, target)


def along_line(value, up=(), down=()):
    def target(x, zl, zh, y, c):
        if zl in up:
            return x, zl + 1, zh, y, c
        if zl in down:
            return x, zl - 1, zh, y, c
        return None

    return move(value, target)


def previous_images(value):
    def target(x, zl, zh, y, c):
        dp = (x * 8 + zl - 1) % 32
        return dp // 8, dp % 8, zh, y, c

    return move(value, target)


def norm_last(values, eps):
    mean = jnp.mean(values, axis=-1, keepdims=True)
    centred = values - mean
    var = jnp.mean(centred * centred, axis=-1, keepdims=True)
    return centred / jnp.sqrt(var + eps)


def norm_kernel(own_ref, other_ref, gain_ref, out_ref):
    parts = [ref[j].astype(jnp.float32) for ref in (own_ref, other_ref) for j in range(8)]
    count = 16 * parts[0].shape[1]
    total = functools.reduce(jnp.add, parts)
    mean = jnp.sum(total, axis=-1, keepdims=True) / count
    parts = [part - mean for part in parts]
    total = functools.reduce(jnp.add, [part * part for part in parts])
    scale = 1.0 / jnp.sqrt(jnp.sum(total, axis=-1, keepdims=True) / count + 1e-06)
    for block, part in enumerate(parts):
        normed = (part * scale * gain_ref[block : block + 1, :]).astype(jnp.bfloat16)
        out_ref[block] = normed[:, :192]
        out_ref[16 + block] = normed[:, 192:]


def norm_tokens(own, other, gain):
    rows = 64
    return pl.pallas_call(
        norm_kernel,
        out_shape=jax.ShapeDtypeStruct((32, 512, 192), jnp.bfloat16),
        grid=(512 // rows,),
        in_specs=[
            pl.BlockSpec((8, rows, 384), lambda i: (0, i, 0)),
            pl.BlockSpec((8, rows, 384), lambda i: (0, i, 0)),
            pl.BlockSpec((16, 384), lambda i: (0, 0)),
        ],
        out_specs=pl.BlockSpec((32, rows, 192), lambda i: (0, i, 0)),
        compiler_params=pltpu.CompilerParams(vmem_limit_bytes=VMEM_LIMIT),
        cost_estimate=pl.CostEstimate(
            flops=512 * 6144 * 8, bytes_accessed=14 * 2**20, transcendentals=0
        ),
    )(own, other, gain)


def add_products(blocks, index_ref, normed_ref, piece_refs, acc_ref):
    for which, (left, right) in blocks:
        rows = normed_ref[index_ref[which]]
        for c in range(3):
            weight = jnp.concatenate(
                [piece_refs[left[0]][left[1], c], piece_refs[right[0]][right[1], c]], axis=-1
            )
            acc_ref[c] += jnp.dot(rows, weight, preferred_element_type=jnp.float32)


def first_kernel(blocks, index_ref, normed_ref, *refs):
    pieces, acc_ref = refs[:-1], refs[-1]
    acc_ref[...] = jnp.zeros_like(acc_ref)
    add_products(blocks, index_ref, normed_ref, pieces, acc_ref)


def next_kernel(blocks, index_ref, normed_ref, held_ref, *refs):
    pieces, acc_ref = refs[:-1], refs[-1]
    acc_ref[...] = held_ref[...]
    add_products(blocks, index_ref, normed_ref, pieces, acc_ref)


def attend(acc_ref, gain_ref, out_ref):
    for head in range(2):
        columns = slice(head * HEAD, (head + 1) * HEAD)
        for image in range(2):
            rows = slice(image * 256, (image + 1) * 256)
            query, keys, values = (
                acc_ref[c, rows, columns].astype(jnp.bfloat16) for c in range(3)
            )
            q_norm = (
                norm_last(query.astype(jnp.float32), 1e-06)
                * gain_ref[0:1, columns]
                * HEAD ** (-0.5)
            ).astype(jnp.bfloat16)
            k_norm = (
                norm_last(keys.astype(jnp.float32), 1e-06) * gain_ref[1:2, columns]
            ).astype(jnp.bfloat16)
            scores = lax.dot_general(
                q_norm, k_norm, (((1,), (1,)), ((), ())), preferred_element_type=jnp.float32
            )
            raised = jnp.exp(scores - jnp.max(scores, axis=-1, keepdims=True))
            probs = (raised / jnp.sum(raised, axis=-1, keepdims=True)).astype(jnp.bfloat16)
            out_ref[rows, columns] = jnp.dot(
                probs, values, preferred_element_type=jnp.float32
            ).astype(jnp.bfloat16)


def last_kernel(blocks, index_ref, normed_ref, held_ref, gain_ref, *refs):
    pieces, out_ref, acc_ref = refs[:-2], refs[-2], refs[-1]
    acc_ref[...] = held_ref[...]
    add_products(blocks, index_ref, normed_ref, pieces, acc_ref)
    attend(acc_ref, gain_ref, out_ref)


def project(kernel, blocks, index, normed, extra, pieces, out_shape, scratch=()):
    whole = pl.BlockSpec(memory_space=pltpu.VMEM)
    return pl.pallas_call(
        functools.partial(kernel, blocks),
        out_shape=out_shape,
        in_specs=[pl.BlockSpec(memory_space=pltpu.SMEM)] + [whole] * (1 + len(extra) + len(pieces)),
        out_specs=whole,
        scratch_shapes=list(scratch),
        compiler_params=pltpu.CompilerParams(vmem_limit_bytes=VMEM_LIMIT),
        cost_estimate=pl.CostEstimate(
            flops=len(blocks) * 512 * 192 * 768 * 2,
            bytes_accessed=8 * 2**20 + len(blocks) * 294912,
            transcendentals=0,
        ),
    )(index, normed, *extra, *pieces)


def relay_kernel(slots, forward, count, zl_ref, *refs):
    sources, rest = refs[:count], refs[count:]
    lefts, rest = rest[: len(forward)], rest[len(forward) :]
    rights, (to_right, to_left) = rest[: len(forward)], rest[-2:]
    zl = zl_ref[0]
    for place, choices in enumerate(slots):
        for source, rows in choices:
            chosen = functools.reduce(jnp.logical_or, [zl == row for row in rows])

            @pl.when(chosen)
            def _(source=source, place=place):
                block = sources[source][...]
                to_right[2 * place : 2 * place + 2] = block
                to_left[2 * place : 2 * place + 2] = block

    end = 2 * len(slots)
    for left_ref, right_ref, blocks in zip(lefts, rights, forward):
        for place in range(blocks):
            to_right[end] = left_ref[2 * place]
            to_left[end] = right_ref[2 * place + 1]
            end += 1


def relay(row, slots, arrays, lefts, rights, forward, after=()):
    whole = pl.BlockSpec(memory_space=pltpu.VMEM)
    message = jax.ShapeDtypeStruct((2 * len(slots) + sum(forward), 3, 192, HEAD), jnp.bfloat16)
    return pl.pallas_call(
        functools.partial(relay_kernel, slots, forward, len(arrays)),
        out_shape=(message, message),
        in_specs=[pl.BlockSpec(memory_space=pltpu.SMEM)]
        + [whole] * (len(arrays) + 2 * len(forward))
        + [pl.BlockSpec(memory_space=pltpu.VMEM)] * len(after),
        out_specs=(whole, whole),
        compiler_params=pltpu.CompilerParams(vmem_limit_bytes=16 * 2**20),
        cost_estimate=pl.CostEstimate(flops=0, bytes_accessed=4 * 2**20, transcendentals=0),
    )(row, *arrays, *lefts, *rights, *after)


def mix_kernel(weight_ref, offset_ref, tokens_ref, partner_ref, *refs):
    mixed_ref = refs[-1]
    for image in range(2):
        lam = weight_ref[image].astype(jnp.float32) / 256.0
        partner = partner_ref[lax.rem(image + offset_ref[image], 2)]
        mixed = lam * tokens_ref[image].astype(jnp.float32) + (1.0 - lam) * partner.astype(
            jnp.float32
        )
        mixed_ref[image] = mixed.astype(jnp.bfloat16)


def mix(weight, offset, tokens, partner, after):
    whole, scalars = pl.BlockSpec(memory_space=pltpu.VMEM), pl.BlockSpec(memory_space=pltpu.SMEM)
    return pl.pallas_call(
        mix_kernel,
        out_shape=jax.ShapeDtypeStruct(tokens.shape, tokens.dtype),
        in_specs=[scalars, scalars, whole, whole]
        + [pl.BlockSpec(memory_space=pltpu.VMEM)] * len(after),
        out_specs=whole,
        compiler_params=pltpu.CompilerParams(vmem_limit_bytes=8 * 2**20),
    )(weight, offset, tokens, partner, *after)


def copy_kernel(count, *refs):
    for source, target in zip(refs[:count], refs[-count:]):
        target[...] = source[...]


def held_back(values, after):
    whole = pl.BlockSpec(memory_space=pltpu.VMEM)
    return pl.pallas_call(
        functools.partial(copy_kernel, len(values)),
        out_shape=[jax.ShapeDtypeStruct(value.shape, value.dtype) for value in values],
        in_specs=[whole] * len(values) + [pl.BlockSpec(memory_space=pltpu.VMEM)] * len(after),
        out_specs=[whole] * len(values),
        compiler_params=pltpu.CompilerParams(vmem_limit_bytes=8 * 2**20),
    )(*values, *after)


def either_kernel(zl_ref, upper_ref, lower_ref, *refs):
    @pl.when(zl_ref[0] >= 4)
    def _():
        refs[-1][...] = upper_ref[...]

    @pl.when(zl_ref[0] < 4)
    def _():
        refs[-1][...] = lower_ref[...]


def either(row, upper, lower, after):
    whole = pl.BlockSpec(memory_space=pltpu.VMEM)
    return pl.pallas_call(
        either_kernel,
        out_shape=jax.ShapeDtypeStruct(upper.shape, upper.dtype),
        in_specs=[pl.BlockSpec(memory_space=pltpu.SMEM), whole, whole]
        + [pl.BlockSpec(memory_space=pltpu.VMEM)] * len(after),
        out_specs=whole,
        compiler_params=pltpu.CompilerParams(vmem_limit_bytes=8 * 2**20),
    )(row, upper, lower, *after)


def per_device(tokens, mix_weight, partner_offset, ln_gain, qkv_weight, qk_gain):
    x, zl, zh = lax.axis_index("x"), lax.axis_index("zl"), lax.axis_index("zh")

    halves = jnp.stack([qkv_weight[:, :, :HEAD], qkv_weight[:, :, HEAD:]])
    partner_block = previous_images(tokens)
    a1 = along_line(halves, up=range(0, 7))
    b1 = along_line(halves, down=range(1, 8))
    sent, left, right = [halves], [along_x(halves, 1)], [along_x(halves, -1)]

    mixed = mix(
        mix_weight, partner_offset, tokens, partner_block, [a1, b1, left[0], right[0]]
    )
    own_features = lax.all_gather(mixed.reshape(512, 384), ("y", "c"))
    halfway = along_z_both_ways(mixed.reshape(512, 384))

    row = zl.reshape(1)

    def send(slots, arrays, forward, after=()):
        lefts = [left[group] for group, _ in forward]
        rights = [right[group] for group, _ in forward]
        to_right, to_left = relay(
            row, slots, arrays, lefts, rights, tuple(blocks for _, blocks in forward), after
        )
        sent.append(to_right)
        left.append(along_x(to_right, 1))
        right.append(along_x(to_left, -1))

    a2 = along_line(a1, up=range(1, 7))
    b2 = along_line(b1, down=range(1, 7))
    send(
        [[(0, range(1, 8)), (3, (0,))], [(1, range(0, 7)), (2, (7,))]],
        [a1, b1, a2, b2],
        [],
    )
    a3 = along_line(a2, up=range(2, 7))
    b3 = along_line(b2, down=range(1, 6))
    (halfway,) = held_back([halfway], [a3, b3])
    other = along_z_both_ways(halfway)
    a4 = along_line(a3, up=range(3, 7))
    b4 = along_line(b3, down=range(1, 5))
    m4 = either(row, a4, b4, [left[1], right[1]])
    send(
        [
            [(0, range(2, 7)), (3, (0, 1)), (4, (7,))],
            [(1, range(1, 6)), (2, (6, 7)), (4, (0,))],
        ],
        [a2, b2, a3, b3, m4],
        [(0, 1)],
    )
    m5 = along_line(m4, up=range(4, 7), down=range(1, 4))
    (other,) = held_back([other], [m5, sent[2]])
    other_features = lax.all_gather(other, ("y", "c"))
    m6 = along_line(m5, up=range(5, 7), down=range(1, 3))
    send(
        [
            [(0, range(1, 7)), (1, (0, 7))],
            [(1, (1, 2, 5, 6)), (2, (0, 7)), (3, (4,)), (4, (3,))],
        ],
        [m4, m5, m6, a3, b3],
        [(1, 2)],
    )
    m7 = along_line(m6, up=(6,), down=(1,))
    send(
        [[(0, (0, 7)), (1, (1, 6)), (2, (3, 5)), (3, (2, 4))]],
        [m7, m6, a3, b3],
        [(2, 2)],
    )

    sources = jnp.asarray(SLOT_SOURCES)[zl]
    block_of = ((x + jnp.arange(4, dtype=jnp.int32)) % 4 * 8)[:, None] + sources[None, :]
    feature = block_of // 2
    index = block_of % 2 * 16 + (feature // 8 + zh) % 2 * 8 + feature % 8
    index = index.reshape(32).astype(jnp.int32)

    gain = ln_gain.reshape(2, 8, 384)
    gain = jnp.where(zh == 0, gain, gain[::-1]).reshape(16, 384)
    normed = norm_tokens(own_features, other_features, gain)

    def three(slot, place):
        return [
            (slot, ((0, 2 * place), (0, 2 * place + 1))),
            (8 + slot, ((2, 2 * place), (2, 2 * place + 1))),
            (24 + slot, ((1, 2 * place), (1, 2 * place + 1))),
        ]

    def at(blocks, base):
        return [
            (which, ((a[0] + base, a[1]), (b[0] + base, b[1]))) for which, (a, b) in blocks
        ]

    def group_blocks(slots_in, opposite):
        blocks = []
        for place, slot in enumerate(slots_in):
            blocks += three(slot, place)
        for place, slot in enumerate(opposite):
            tail = 2 * len(slots_in) + place
            blocks.append((16 + slot, ((1, tail), (2, tail))))
        return blocks

    def arrays(group):
        return [sent[group], left[group], right[group]]

    first_blocks, pieces = [], []
    for group, (slots_in, opposite) in enumerate(
        [((0,), ()), ((1, 2), ()), ((3, 4), (0,)), ((5, 6), (1, 2))]
    ):
        first_blocks += at(group_blocks(slots_in, opposite), 3 * group)
        pieces += arrays(group)
    acc_shape = jax.ShapeDtypeStruct((3, 512, 256), jnp.float32)
    acc = project(first_kernel, first_blocks, index, normed, [], pieces, acc_shape)
    send([], [], [(3, 2), (4, 1)], [acc])
    acc = project(
        next_kernel, group_blocks((7,), (3, 4)), index, normed, [acc], arrays(4), acc_shape
    )
    out = project(
        last_kernel,
        at(group_blocks((), (5, 6, 7)), -1),
        index,
        normed,
        [acc, qk_gain],
        arrays(5)[1:],
        jax.ShapeDtypeStruct((512, 256), jnp.bfloat16),
        [pltpu.VMEM((3, 512, 256), jnp.float32)],
    )
    return out.reshape(2, 256, 256)


def solution(mesh):
    grid = Mesh(mesh.devices.reshape(SIZES), AXES)
    dp, tensor = ("x", "zl"), ("zh", "y", "c")
    placed = (
        P(dp, None, tensor),
        P(dp),
        P(dp),
        P(),
        P(None, dp, tensor),
        P(None, tensor),
    )
    return jax.shard_map(
        per_device, mesh=grid, in_specs=placed, out_specs=P(dp, None, tensor), check_vma=False
    )
```
